32 devices in a mesh: sub: 16 (over z, y, x), sep: 2 (over core).
Axes of the slice: x: 2, y: 2, z: 4, core: 2. Of those that a mesh axis runs over, the one named last changes fastest.
Arguments:
- sources: bfloat16 [16, 2, 768, 256], P('sub', 'sep'), may hold values from -6 to 6
- inner_inv: bfloat16 [16, 2, 768, 768], P('sub', 'sep'), as said below
- coupling: bfloat16 [16, 2, 512, 768], P('sub', 'sep'), may hold values from -0.0546875 to 0.0546875
- boundary_map: int32 [16, 2, 512], P('sub', 'sep'), may hold values from 0 to 479, as said below
- sep_inv_0: bfloat16 [16, 64, 64], P('sub', 'sep'), as said below
- sep_inv_1: bfloat16 [16, 128, 128], P('sub', 'sep'), as said below
- sep_inv_2: bfloat16 [16, 256, 256], P('sub', 'sep'), as said below
- sep_inv_3: bfloat16 [16, 512, 512], P('sub', 'sep'), as said below
- sep_couple_0: bfloat16 [16, 128, 64], P('sub', 'sep'), as said below
- sep_couple_1: bfloat16 [16, 256, 128], P('sub', 'sep'), as said below
- sep_couple_2: bfloat16 [16, 512, 256], P('sub', 'sep'), as said below
Outputs:
- inner_solution: bfloat16 [16, 2, 768, 256], P('sub', 'sep')
- sep_solution: bfloat16 [16, 2, 480, 256], P('sub', 'sep')
The draws below stay inside these ranges and needn't reach their ends.
Inputs may be any that keep to these rules, and one draw needn't show every extreme that they name: `boundary_map`: an entry m with (2^l - 1) * 32 <= m < (2^(l+1) - 1) * 32 names row m - (2^l - 1) * 32 of the leaf's own strip in the level-l separator above its subdomain. Every inner_inv[s, p] is lower triangular with a positive diagonal. Every sep_inv_0[s] is lower triangular with a positive diagonal, and equal for all s of one level-0 group. Every sep_inv_1[s] is lower triangular with a positive diagonal, and equal for all s of one level-1 group. Every sep_inv_2[s] is lower triangular with a positive diagonal, and equal for all s of one level-2 group. Every sep_inv_3[s] is lower triangular with a positive diagonal, and equal for all s of one level-3 group. sep_couple_0[s] is equal for all s of one level-0 group. sep_couple_1[s] is equal for all s of one level-1 group. sep_couple_2[s] is equal for all s of one level-2 group.
All inputs are finite; a program needn't handle non-finite values.
Results may differ from the reference program's by a relative error of at most 0.017.
Values may be sent and summed in bfloat16 or wider, within the bound.
No kernel may reach another device: no remote copies, remote signals or barrier semaphores. Data moves between devices by JAX's collectives and lax.ppermute only.
A program may use at most 64 MiB of HBM per device.

```python
import math
import jax
import jax.numpy as jnp
from jax import lax

INNER = 768
BOUNDARY = 512
ROWS_0 = 32
SHOTS = 256
LEVELS = 4
SUBS = 16
STRIPS = 2
ORDER_0 = 64
ORDER_1 = 128
ORDER_2 = 256
ORDER_3 = 512
TOTAL_ROWS = 480


def lower_factor(key_lower, key_diagonal, leading, order):
    row_index = lax.broadcasted_iota(jnp.int32, (order, order), 0)
    col_index = lax.broadcasted_iota(jnp.int32, (order, order), 1)
    strict_lower = jnp.clip(jax.random.normal(key_lower, leading + (order, order), jnp.float32), -4.0, 4.0)
    diagonal = jax.random.uniform(key_diagonal, leading + (order, 1), jnp.float32, 0.5, 1.5)
    scaled = strict_lower * (0.8 / math.sqrt(order))
    return jnp.where(row_index > col_index, scaled, jnp.where(row_index == col_index, diagonal, 0.0))


def draw_inner_inv(key, part):
    base_key = jax.random.fold_in(key, 101)

    def draw_sub(index):
        sub_key = jax.random.fold_in(base_key, index)
        key_lower, key_diagonal = jax.random.split(sub_key)
        return lower_factor(key_lower, key_diagonal, (STRIPS,), INNER)
    return lax.map(draw_sub, jnp.arange(SUBS, dtype=jnp.int32)).astype(jnp.bfloat16)


def separator_level(key, height, order):
    members = min(4 ** (height + 1), SUBS)
    level_key = jax.random.fold_in(key, 200 + height)
    key_lower, key_diagonal = jax.random.split(level_key)
    blocks = lower_factor(key_lower, key_diagonal, (SUBS // members,), order)
    return jnp.repeat(blocks, members, axis=0)


def couple_level(key, height, parent_order, child_order):
    members = min(4 ** (height + 1), SUBS)
    level_key = jax.random.fold_in(key, 300 + height)
    block_shape = (SUBS // members, parent_order, child_order)
    dense = jnp.clip(jax.random.normal(level_key, block_shape, jnp.float32), -4.0, 4.0) * (0.35 / math.sqrt(child_order))
    return jnp.repeat(dense, members, axis=0)


def draw_sep_inv_0(key, part):
    return separator_level(key, 0, ORDER_0).astype(jnp.bfloat16)


def draw_sep_inv_1(key, part):
    return separator_level(key, 1, ORDER_1).astype(jnp.bfloat16)


def draw_sep_inv_2(key, part):
    return separator_level(key, 2, ORDER_2).astype(jnp.bfloat16)


def draw_sep_inv_3(key, part):
    return separator_level(key, 3, ORDER_3).astype(jnp.bfloat16)


def draw_sep_couple_0(key, part):
    return couple_level(key, 0, ORDER_1, ORDER_0).astype(jnp.bfloat16)


def draw_sep_couple_1(key, part):
    return couple_level(key, 1, ORDER_2, ORDER_1).astype(jnp.bfloat16)


def draw_sep_couple_2(key, part):
    return couple_level(key, 2, ORDER_3, ORDER_2).astype(jnp.bfloat16)


def draw_boundary_map(key, part):
    row_key = jax.random.fold_in(key, 401)
    return jax.random.randint(row_key, (SUBS, STRIPS, BOUNDARY), 0, TOTAL_ROWS, dtype=jnp.int32)


def steps_of(stream_key, extent, cuts, smallest, largest):
    level, own = 1.0, jax.random.fold_in(stream_key, 6)
    for dim, shards_of in cuts:
        draws = jnp.exp(jax.random.uniform(jax.random.fold_in(own, dim), (shards_of,), jnp.float32, smallest / len(cuts), largest / len(cuts)))
        level = level * jnp.repeat(draws, extent[dim] // shards_of).reshape([-1 if axis == dim else 1 for axis in range(len(extent))])
    return level


def gaussian(rng, shape, deviation, bound, cuts=(), held_as=jnp.bfloat16):
    values = deviation * jax.random.normal(rng, shape, jnp.float32)
    if cuts:
        values = values * steps_of(rng, shape, cuts, -0.22, 0.18)
    return jnp.clip(values, -bound, bound).astype(held_as)


def setup_inputs(seed: int = 0) -> dict:
    splits = jax.random.split(jax.random.key(seed), 12)
    return {
        "sources": gaussian(splits[0], (SUBS, STRIPS, INNER, SHOTS), 1.0, 6.0, ((0, 16), (1, 2))),
        "inner_inv": draw_inner_inv(jax.random.fold_in(splits[11], 71), 0),
        "coupling": gaussian(splits[2], (SUBS, STRIPS, BOUNDARY, INNER), (16 * INNER) ** -0.5, 0.0546875, ((0, 16), (1, 2))),
        "boundary_map": draw_boundary_map(jax.random.fold_in(splits[11], 71), 0),
        "sep_inv_0": draw_sep_inv_0(jax.random.fold_in(splits[11], 71), 0),
        "sep_inv_1": draw_sep_inv_1(jax.random.fold_in(splits[11], 71), 0),
        "sep_inv_2": draw_sep_inv_2(jax.random.fold_in(splits[11], 71), 0),
        "sep_inv_3": draw_sep_inv_3(jax.random.fold_in(splits[11], 71), 0),
        "sep_couple_0": draw_sep_couple_0(jax.random.fold_in(splits[11], 71), 0),
        "sep_couple_1": draw_sep_couple_1(jax.random.fold_in(splits[11], 71), 0),
        "sep_couple_2": draw_sep_couple_2(jax.random.fold_in(splits[11], 71), 0),
    }


def group_size(height):
    return min(4 ** (height + 1), SUBS)


def leaf_forward(pieces):
    source_rows, inverse, couple, targets = pieces
    inner_half = jnp.einsum('pik,pkn->pin', inverse.astype(jnp.float32), source_rows.astype(jnp.float32)).astype(jnp.bfloat16)
    boundary_half = jnp.einsum('pbk,pkn->pbn', couple.astype(jnp.float32), inner_half.astype(jnp.float32)).astype(jnp.bfloat16)
    slot_ids = jnp.arange(TOTAL_ROWS, dtype=jnp.int32)
    onehot = (targets[:, None, :] == slot_ids[None, :, None]).astype(jnp.float32)
    leaf_rows = jnp.einsum('prb,pbn->prn', onehot, boundary_half.astype(jnp.float32))
    return inner_half, leaf_rows


def leaf_backward(pieces):
    own_rows, targets, couple, inverse, inner_half = pieces
    picked = jax.vmap(lambda matrix, picks: jnp.take(matrix, picks, axis=0))(own_rows, targets)
    lifted = jnp.einsum('pbk,pbn->pkn', couple.astype(jnp.float32), picked.astype(jnp.float32)).astype(jnp.bfloat16)
    direct = jnp.einsum('pik,pin->pkn', inverse.astype(jnp.float32), inner_half.astype(jnp.float32))
    correction = jnp.einsum('pik,pin->pkn', inverse.astype(jnp.float32), lifted.astype(jnp.float32))
    return (direct - correction).astype(jnp.bfloat16)


def reference(sources, inner_inv, coupling, boundary_map, sep_inv_0, sep_inv_1, sep_inv_2, sep_inv_3, sep_couple_0, sep_couple_1, sep_couple_2):
    separators = [sep_inv_0, sep_inv_1, sep_inv_2, sep_inv_3]
    parents = [sep_couple_0, sep_couple_1, sep_couple_2]
    inner_half, leaf_rows = lax.map(leaf_forward, (sources, inner_inv, coupling, boundary_map))
    forward_rows = []
    child_term = None
    for height in range(LEVELS):
        size = ROWS_0 * 2 ** height
        start = ROWS_0 * (2 ** height - 1)
        members = group_size(height)
        groups = SUBS // members
        block = leaf_rows[:, :, start:start + size]
        rhs_rows = block.reshape(groups, members, STRIPS * size, SHOTS).sum(axis=1)
        if child_term is not None:
            rhs_rows = rhs_rows + child_term.reshape(groups, -1, STRIPS * size, SHOTS).sum(axis=1)
        rhs_half = rhs_rows.astype(jnp.bfloat16)
        matrix = separators[height][::members].astype(jnp.float32)
        solved = jnp.einsum('grk,gkn->grn', matrix, rhs_half.astype(jnp.float32)).astype(jnp.bfloat16)
        forward_rows.append(solved)
        if height < LEVELS - 1:
            child_term = jnp.einsum('grk,gkn->grn', parents[height][::members].astype(jnp.float32), solved.astype(jnp.float32))
    backward_rows = [None] * LEVELS
    for height in reversed(range(LEVELS)):
        members = group_size(height)
        matrix = separators[height][::members].astype(jnp.float32)
        if height == LEVELS - 1:
            target = forward_rows[height]
        else:
            fanout = group_size(height + 1) // members
            parent = jnp.repeat(backward_rows[height + 1], fanout, axis=0)
            back_term = jnp.einsum('grk,grn->gkn', parents[height][::members].astype(jnp.float32), parent.astype(jnp.float32))
            target = (forward_rows[height].astype(jnp.float32) - back_term).astype(jnp.bfloat16)
        backward_rows[height] = jnp.einsum('grk,grn->gkn', matrix, target.astype(jnp.float32)).astype(jnp.bfloat16)
    pieces = []
    for height in range(LEVELS):
        size = ROWS_0 * 2 ** height
        spread = jnp.repeat(backward_rows[height], group_size(height), axis=0)
        pieces.append(spread.reshape(SUBS, STRIPS, size, SHOTS))
    sep_solution = jnp.concatenate(pieces, axis=2)
    inner_solution = lax.map(leaf_backward, (sep_solution, boundary_map, coupling, inner_inv, inner_half))
    return (inner_solution, sep_solution)
```

```python
import jax
import jax.numpy as jnp
from jax import lax
from jax.experimental import pallas as pl
from jax.experimental.pallas import tpu as pltpu
from jax.sharding import PartitionSpec as P

BLOCK = 256
CHIPS = 4
MIB = 1024 * 1024
VMEM = pl.BlockSpec(memory_space=pltpu.VMEM)
SMEM = pl.BlockSpec(memory_space=pltpu.SMEM)
HBM = pl.BlockSpec(memory_space=pltpu.HBM)


def bf16(x):
    return x.astype(jnp.bfloat16)


def dot(a, b):
    return jnp.dot(a, b, preferred_element_type=jnp.float32)


def dot_tn(a, b):
    return lax.dot_general(a, b, (((0,), (0,)), ((), ())), preferred_element_type=jnp.float32)


def call(kernel, name, outs, ins, specs, out_specs, flops, limit=16, scratch=()):
    ins = [pltpu.with_memory_space_constraint(x, pltpu.HBM) if s is HBM else x for x, s in zip(ins, specs)]
    moved = sum(x.size * x.dtype.itemsize for x in ins)
    return pl.pallas_call(
        kernel,
        out_shape=outs,
        in_specs=specs,
        out_specs=out_specs,
        scratch_shapes=list(scratch),
        compiler_params=pltpu.CompilerParams(vmem_limit_bytes=limit * MIB),
        cost_estimate=pl.CostEstimate(flops=flops, bytes_accessed=moved, transcendentals=0),
        name=name,
    )(*ins)


def struct(shape, dtype=jnp.bfloat16):
    return jax.ShapeDtypeStruct(shape, dtype)


def offsets(sizes):
    return [sum(sizes[:i]) for i in range(len(sizes))]


def places(sizes):
    return [sum(sizes[i + 1 :]) for i in range(len(sizes))]


def scatter_matrix(tgt, sizes):
    moved = tgt
    for start, place, size in zip(offsets(sizes), places(sizes), sizes):
        inside = (tgt >= start) & (tgt < start + size)
        moved = jnp.where(inside, tgt + (place - start), moved)
    slots = lax.broadcasted_iota(jnp.int32, (sum(sizes), tgt.shape[1]), 0)
    return bf16(jnp.where(slots == moved, 1.0, 0.0))


def leaf_forward(src, inv, cpl, tgt, separators, parents):
    inner, shots = src.shape
    count = inner // BLOCK
    sizes = [m.shape[0] for m in separators]
    s0, s1, s2, s3 = sizes
    o0, o1, o2, o3 = [m.shape[1] for m in separators]

    def kernel(src_hbm, inv_hbm, cpl_hbm, tgt_hbm, i0, i1, i2, i3, c0, c1, c2,
               half_ref, rows_ref, pack_ref, src, inv, cpl, edge_ref, small0, small1, tgt_ref, sems):
        copies = []
        for i in range(count):
            rows = pl.ds(i * BLOCK, BLOCK)
            cols = pl.ds(0, (i + 1) * BLOCK)
            group = [
                pltpu.make_async_copy(src_hbm.at[rows], src.at[rows], sems.at[3 * i]),
                pltpu.make_async_copy(inv_hbm.at[rows, cols], inv.at[rows, cols], sems.at[3 * i + 1]),
                pltpu.make_async_copy(cpl_hbm.at[:, rows], cpl.at[:, rows], sems.at[3 * i + 2]),
            ]
            for copy in group:
                copy.start()
            copies.append(group)
        base = 3 * count
        packs = [
            (i3, pack_ref.at[pl.ds(0, s3), :]),
            (c2, pack_ref.at[pl.ds(s3, s3), pl.ds(0, o2)]),
            (i2, pack_ref.at[pl.ds(s3, s2), pl.ds(o2, o2)]),
            (c1, pack_ref.at[pl.ds(s3 + s2, s2), pl.ds(o2, o1)]),
            (i1, pack_ref.at[pl.ds(s3 + s2, s1), pl.ds(o2 + o1, o1)]),
        ]
        packs += [(i0, small0), (c0, small1), (tgt_hbm, tgt_ref)]
        packs = [pltpu.make_async_copy(a, b, sems.at[base + i]) for i, (a, b) in enumerate(packs)]
        for copy in reversed(packs):
            copy.start()
        for copy in packs[-3:]:
            copy.wait()
        pack_ref[pl.ds(2 * s3, s0), pl.ds(0, o0)] = small0[...]
        pack_ref[pl.ds(s3 + s2 + s1, s1), pl.ds(o2 + o1, o0)] = small1[...]
        onehot = scatter_matrix(tgt_ref[...], sizes)
        for i in range(count):
            rows = pl.ds(i * BLOCK, BLOCK)
            cols = pl.ds(0, (i + 1) * BLOCK)
            copies[i][0].wait()
            copies[i][1].wait()
            half = bf16(dot(inv[rows, cols], src[cols, :]))
            half_ref[rows, :] = half
            copies[i][2].wait()
            term = dot(cpl[:, rows], half)
            if i == 0:
                edge_ref[...] = term
            else:
                edge_ref[...] += term
        rows_ref[...] = bf16(dot(onehot, bf16(edge_ref[...])))
        for copy in packs[:-3]:
            copy.wait()

    return call(
        kernel,
        "leaf_forward",
        (
            struct((inner, shots)),
            struct((sum(sizes), shots)),
            struct((2 * s3 + s0, o3)),
        ),
        (src, inv, cpl, tgt, *separators, *parents),
        [HBM] * 11,
        (VMEM, VMEM, VMEM),
        600_000_000,
        scratch=[
            pltpu.VMEM(src.shape, jnp.bfloat16),
            pltpu.VMEM(inv.shape, jnp.bfloat16),
            pltpu.VMEM(cpl.shape, jnp.bfloat16),
            pltpu.VMEM((cpl.shape[0], shots), jnp.float32),
            pltpu.VMEM((s0, o0), jnp.bfloat16),
            pltpu.VMEM((s1, o0), jnp.bfloat16),
            pltpu.VMEM(tgt.shape, jnp.int32),
            pltpu.SemaphoreType.DMA((3 * count + 8,)),
        ],
    )


def ordered(first, own, other):
    return jnp.concatenate([jnp.where(first, own, other), jnp.where(first, other, own)], 0)


def shares(sizes):
    s0, s1, s2, s3 = sizes
    return (s3 + s2 + 2 * s1) // CHIPS, s0 // 2


def fold_lowest(where, rows, small, far_small, sizes):
    s0, s1, s2, s3 = sizes
    main, side = shares(sizes)
    total = sum(sizes)

    def kernel(where_ref, rows_ref, inv_ref, cpl_ref, far_inv_ref, far_cpl_ref, *outs):
        out_refs, buf = outs[:CHIPS], outs[CHIPS]
        first = where_ref[0] == 0
        inv = ordered(first, inv_ref[...], far_inv_ref[...])
        lowest = rows_ref[pl.ds(total - s0, s0), :]
        up = bf16(dot(inv, ordered(first, lowest, jnp.zeros_like(lowest))))
        own = rows_ref[pl.ds(s3 + s2, s1), :].astype(jnp.float32) + dot(cpl_ref[...], up)
        far = dot(far_cpl_ref[...], up)
        folded = [rows_ref[pl.ds(0, s3 + s2), :], bf16(own), bf16(far)]
        folded = jnp.concatenate(folded, 0)
        for q in range(CHIPS):
            buf[q, pl.ds(0, main), :] = folded[q * main : (q + 1) * main]
            if q < 2:
                buf[q, pl.ds(main, side), :] = lowest[q * side : (q + 1) * side]
            else:
                buf[q, pl.ds(main, side), :] = jnp.zeros((side, rows.shape[1]), jnp.bfloat16)
        for k in range(CHIPS):
            out_refs[k][...] = buf[where_ref[1] ^ k]

    share = struct((main + side, rows.shape[1]))
    return call(
        kernel,
        "fold_lowest",
        (share,) * CHIPS,
        (where, rows, *small, *far_small),
        [SMEM] + [VMEM] * 5,
        (VMEM,) * CHIPS,
        10_000_000,
        limit=4,
        scratch=[pltpu.VMEM((CHIPS, main + side, rows.shape[1]), jnp.bfloat16)],
    )


def solve_operator(strip, pack, far_pack, separators, parents):
    s = [m.shape[0] for m in separators]
    o = [m.shape[1] for m in separators]
    total = sum(s)

    def kernel(strip_ref, own_ref, far_ref, out_ref):
        first = strip_ref[0] == 0

        def whole(row, rows, col, cols):
            at = (pl.ds(row, rows), pl.ds(col, cols))
            return ordered(first, own_ref[at], far_ref[at])

        x3 = whole(0, s[3], 0, o[3])
        c2 = whole(s[3], s[3], 0, o[2])
        x2 = whole(s[3], s[2], o[2], o[2])
        c1 = whole(s[3] + s[2], s[2], o[2], o[1])
        x1 = whole(s[3] + s[2], s[1], o[2] + o[1], o[1])
        c0 = whole(s[3] + s[2] + s[1], s[1], o[2] + o[1], o[0])
        x0 = whole(2 * s[3], s[0], 0, o[0])
        t3 = bf16(dot(x3, c2))
        t2 = bf16(dot(x2, c1))
        t1 = bf16(dot(x1, c0))
        n32 = bf16(dot(t3, x2))
        n21 = bf16(dot(t2, x1))
        n10 = bf16(dot(t1, x0))
        n31 = bf16(dot(t3, n21))
        n20 = bf16(dot(t2, n10))
        n30 = bf16(dot(t3, n20))

        def turned(x, sign):
            y = x.astype(jnp.float32).T
            half = y.shape[0] // 2
            return bf16(sign * jnp.where(first, y[:half], y[half:]))

        m3 = jnp.concatenate([turned(x3, 1.0), turned(n32, -1.0), turned(n31, 1.0), turned(n30, -1.0)], 0)
        m2 = jnp.concatenate([turned(x2, 1.0), turned(n21, -1.0), turned(n20, 1.0)], 0)
        m1 = jnp.concatenate([turned(x1, 1.0), turned(n10, -1.0)], 0)
        m0 = turned(x0, 1.0)
        top, mid, low = s[3], s[3] + s[2], s[3] + s[2] + s[1]
        a, b, c = o[3], o[3] + o[2], o[3] + o[2] + o[1]
        out_ref[:, pl.ds(0, a)] = bf16(dot(m3, x3))
        second = dot(m3, n32)
        out_ref[pl.ds(0, top), pl.ds(a, o[2])] = bf16(second[:top])
        out_ref[pl.ds(top, total - top), pl.ds(a, o[2])] = bf16(second[top:] + dot(m2, x2))
        third = dot(m3, n31)
        out_ref[pl.ds(0, top), pl.ds(b, o[1])] = bf16(third[:top])
        rest = third[top:] + dot(m2, n21)
        out_ref[pl.ds(top, s[2]), pl.ds(b, o[1])] = bf16(rest[: s[2]])
        out_ref[pl.ds(mid, total - mid), pl.ds(b, o[1])] = bf16(rest[s[2] :] + dot(m1, x1))
        out_ref[pl.ds(0, low), pl.ds(c, o[0])] = jnp.zeros((low, o[0]), jnp.bfloat16)
        out_ref[pl.ds(low, s[0]), pl.ds(c, o[0])] = bf16(dot(m0, x0))

    return call(
        kernel,
        "solve_operator",
        struct((total, sum(o))),
        (strip, pack, far_pack),
        [SMEM, VMEM, VMEM],
        VMEM,
        1_000_000_000,
    )


def leaf_backward(inv, cpl, tgt, half, sizes):
    inner, shots = half.shape
    count = inner // BLOCK
    total = sum(sizes)

    def kernel(inv_ref, cpl_ref, tgt_ref, half_ref, direct_ref, lift_ref, reach_ref):
        onehot = scatter_matrix(tgt_ref[...], sizes)
        for i in range(count):
            cols = pl.ds(i * BLOCK, BLOCK)
            reach_ref[:, cols] = bf16(dot(onehot, cpl_ref[:, cols]))
        for j in range(count):
            rows = pl.ds(j * BLOCK, inner - j * BLOCK)
            cols = pl.ds(j * BLOCK, BLOCK)
            block = inv_ref[rows, cols]
            direct_ref[cols, :] = dot_tn(block, half_ref[rows, :])
            lift_ref[cols, :] = bf16(dot(reach_ref[:, rows], block).T)

    return call(
        kernel,
        "leaf_backward",
        (struct((inner, shots), jnp.float32), struct((inner, total))),
        (inv, cpl, tgt, half),
        [VMEM] * 4,
        (VMEM, VMEM),
        1_000_000_000,
        scratch=[pltpu.VMEM((total, inner), jnp.bfloat16)],
    )


def finish(where, shared, far_shared, solve, lift, direct, sizes):
    s0, s1, s2, s3 = sizes
    main, side = shares(sizes)
    each = main + side
    total = sum(sizes)
    shots = shared.shape[1]

    def kernel(where_ref, own_ref, far_ref, solve_ref, lift_ref, direct_ref, inner_ref, sep_ref, own_buf, far_buf, rhs):
        first = where_ref[0] == 0
        for k in range(CHIPS):
            q = where_ref[1] ^ k
            own_buf[q] = own_ref[pl.ds(k * each, each), :]
            far_buf[q] = far_ref[pl.ds(k * each, each), :]

        def put(at, span, own, far):
            size = own.shape[0]
            rhs[pl.ds(at, size), :] = jnp.where(first, own, far)
            rhs[pl.ds(at + span, size), :] = jnp.where(first, far, own)

        def pieces(start, size):
            while size > 0:
                q, low = divmod(start, main)
                count = min(size, main - low)
                yield q, low, count
                start, size = start + count, size - count

        start = at = 0
        for span in (s3, s2):
            for q, low, count in pieces(start, span):
                put(at, span, own_buf[q, pl.ds(low, count), :], far_buf[q, pl.ds(low, count), :])
                at += count
            at += span
            start += span
        for (q, low, count), (q2, low2, _) in zip(pieces(start, s1), pieces(start + s1, s1)):
            own, far = [b[q, pl.ds(low, count), :].astype(jnp.float32) for b in (own_buf, far_buf)]
            own2, far2 = [b[q2, pl.ds(low2, count), :].astype(jnp.float32) for b in (own_buf, far_buf)]
            put(at, s1, bf16(own + far2), bf16(far + own2))
            at += count
        at += s1
        for q in range(2):
            put(at, s0, own_buf[q, pl.ds(main, side), :], far_buf[q, pl.ds(main, side), :])
            at += side
        down = bf16(dot(solve_ref[...], rhs[...]))
        for begin, place, size in zip(offsets(sizes), places(sizes), sizes):
            sep_ref[pl.ds(begin, size), :] = down[place : place + size]
        inner_ref[...] = bf16(direct_ref[...] - dot(lift_ref[...], down))

    return call(
        kernel,
        "finish",
        (struct(direct.shape), struct((total, shots))),
        (where, shared, far_shared, solve, lift, direct),
        [SMEM] + [VMEM] * 5,
        (VMEM, VMEM),
        500_000_000,
        scratch=[
            pltpu.VMEM((CHIPS, each, shots), jnp.bfloat16),
            pltpu.VMEM((CHIPS, each, shots), jnp.bfloat16),
            pltpu.VMEM((2 * total, shots), jnp.bfloat16),
        ],
    )


def other_strip(x):
    return lax.ppermute(x, "sep", [(0, 1), (1, 0)])


def partner(x, mask):
    return lax.ppermute(x, "sub", [(s, s ^ mask) for s in range(lax.axis_size("sub"))])


def added(*terms):
    return bf16(sum(t.astype(jnp.float32) for t in terms))


def local(sources, inner_inv, coupling, boundary_map, *blocks):
    src, inv, cpl, tgt = sources[0, 0], inner_inv[0, 0], coupling[0, 0], boundary_map[0]
    separators = [m[0] for m in blocks[:4]]
    parents = [m[0] for m in blocks[4:]]
    sizes = [m.shape[0] for m in separators]
    main, _ = shares(sizes)
    sub = lax.axis_index("sub")
    where = jnp.stack([lax.axis_index("sep"), lax.rem(sub, CHIPS)]).astype(jnp.int32)
    small = (separators[0], parents[0])
    far_small = tuple(other_strip(m) for m in small)
    half, rows, pack = leaf_forward(src, inv, cpl, tgt, separators, parents)
    parts = fold_lowest(where, rows, small, far_small, sizes)
    share = added(parts[0], *[partner(parts[k], k) for k in range(1, CHIPS)])
    direct, lift = leaf_backward(inv, cpl, tgt, half, sizes)
    far_pack = other_strip(pack)
    solve = solve_operator(where, pack, far_pack, separators, parents)
    top = share[:main]
    along = [partner(top, CHIPS * k) for k in range(1, CHIPS)]
    along, direct, lift, solve = lax.optimization_barrier((along, direct, lift, solve))
    share = jnp.concatenate([added(top, *along), share[main:]], 0)
    shared = jnp.concatenate([share] + [partner(share, k) for k in range(1, CHIPS)], 0)
    inner, sep = finish(where, shared, other_strip(shared), solve, lift, direct, sizes)
    return (inner[None, None], sep[None, None])


def local_any(sources, inner_inv, coupling, boundary_map, *blocks):
    src, inv, cpl, tgt = sources[0, 0], inner_inv[0, 0], coupling[0, 0], boundary_map[0, 0]
    separators = [m[0] for m in blocks[:4]]
    parents = [m[0] for m in blocks[4:]]
    sizes = [m.shape[0] for m in separators]
    levels = len(sizes)
    bits = lax.axis_size("sub").bit_length() - 1

    def both(x):
        return lax.all_gather(x, "sep", axis=0, tiled=True)

    half = bf16(dot(inv, src))
    edge = bf16(dot(cpl, half))
    slots = lax.broadcasted_iota(jnp.int32, (sum(sizes), tgt.shape[0]), 0)
    carried = dot(bf16(slots == tgt[None, :]), edge)
    ups = []
    for level, size in enumerate(sizes):
        for bit in range(2 * level, min(2 * level + 2, bits)):
            sent = partner(bf16(carried), 1 << bit)
            carried = carried + sent.astype(jnp.float32)
        up = both(bf16(dot(separators[level], both(bf16(carried[:size])))))
        ups.append(up)
        carried = carried[size:]
        if level < levels - 1:
            carried = carried.at[: sizes[level + 1]].add(dot(parents[level], up))
    own, down = [None] * levels, None
    for level in reversed(range(levels)):
        target = ups[level]
        if down is not None:
            target = bf16(target.astype(jnp.float32) - dot_tn(both(parents[level]), down))
        down = bf16(dot_tn(both(separators[level]), target))
        own[level] = lax.dynamic_slice_in_dim(down, lax.axis_index("sep") * sizes[level], sizes[level], 0)
    sep = jnp.concatenate(own, 0)
    lifted = bf16(dot_tn(cpl, jnp.take(sep, tgt, axis=0)))
    inner = bf16(dot_tn(inv, half) - dot_tn(inv, lifted))
    return (inner[None, None], sep[None, None])


def solution(mesh):
    whole = P("sub", "sep", None, None)
    placed = (whole,) * 2 + (whole, P("sub", "sep", None)) + (P("sub", "sep", None),) * 7
    two_stages = mesh.shape["sub"] == CHIPS * CHIPS
    return jax.shard_map(
        local if two_stages else local_any,
        mesh=mesh,
        in_specs=placed,
        out_specs=(whole, whole),
        check_vma=False,
    )
```

```python
import jax
import jax.numpy as jnp
from jax import lax
from jax.experimental import pallas as pl
from jax.experimental.pallas import tpu as pltpu
from jax.sharding import PartitionSpec as P

BLOCK = 256
CHIPS = 4
MIB = 1024 * 1024
VMEM = pl.BlockSpec(memory_space=pltpu.VMEM)
HBM = pl.BlockSpec(memory_space=pltpu.HBM)


def bf16(x):
    return x.astype(jnp.bfloat16)


def dot(a, b):
    return jnp.dot(a, b, preferred_element_type=jnp.float32)


def dot_tn(a, b):
    return lax.dot_general(a, b, (((0,), (0,)), ((), ())), preferred_element_type=jnp.float32)


def call(kernel, name, outs, ins, specs, out_specs, flops, limit=16, scratch=()):
    ins = [pltpu.with_memory_space_constraint(x, pltpu.HBM) if s is HBM else x for x, s in zip(ins, specs)]
    moved = sum(x.size * x.dtype.itemsize for x in ins)
    return pl.pallas_call(
        kernel,
        out_shape=outs,
        in_specs=specs,
        out_specs=out_specs,
        scratch_shapes=list(scratch),
        compiler_params=pltpu.CompilerParams(vmem_limit_bytes=limit * MIB),
        cost_estimate=pl.CostEstimate(flops=flops, bytes_accessed=moved, transcendentals=0),
        name=name,
    )(*ins)


def in_plane():
    return lax.rem(lax.axis_index("sub"), CHIPS)


def struct(shape, dtype=jnp.bfloat16):
    return jax.ShapeDtypeStruct(shape, dtype)


def offsets(sizes):
    return [sum(sizes[:i]) for i in range(len(sizes))]


def places(sizes):
    return [sum(sizes[i + 1 :]) for i in range(len(sizes))]


def moved_rows(tgt, sizes, order):
    moved = tgt
    for start, place, size in zip(offsets(sizes), order, sizes):
        inside = (tgt >= start) & (tgt < start + size)
        moved = jnp.where(inside, tgt + (place - start), moved)
    return moved


def scatter_matrix(moved, rows, start=0):
    slots = lax.broadcasted_iota(jnp.int32, (rows, moved.shape[1]), 0)
    return bf16(jnp.where(slots + start == moved, 1.0, 0.0))


def leaf_forward(src, inv, cpl, tgt, separators, parents):
    inner, shots = src.shape
    count = inner // BLOCK
    sizes = [m.shape[0] for m in separators]
    s0, s1, s2, s3 = sizes
    o0, o1, o2, o3 = [m.shape[1] for m in separators]
    part, _ = share_rows(sizes)

    def kernel(src_hbm, inv_hbm, cpl_hbm, tgt_hbm, i0, i1, i2, i3, c0, c1, c2,
               half_ref, share0, share1, share2, share3, pack_ref,
               src, inv, cpl, edge_ref, small0, small1, tgt_ref, sems):
        moves = [(tgt_hbm, tgt_ref)]
        for i in range(count):
            rows = pl.ds(i * BLOCK, BLOCK)
            cols = pl.ds(0, (i + 1) * BLOCK)
            moves.append((src_hbm.at[rows], src.at[rows]))
            moves.append((inv_hbm.at[rows, cols], inv.at[rows, cols]))
            moves.append((cpl_hbm.at[:, rows], cpl.at[:, rows]))
        leaf = len(moves)
        moves += [
            (i0, small0),
            (c0, small1),
            (i3, pack_ref.at[pl.ds(0, s3), :]),
            (c2, pack_ref.at[pl.ds(s3, s3), pl.ds(0, o2)]),
            (i2, pack_ref.at[pl.ds(s3, s2), pl.ds(o2, o2)]),
            (c1, pack_ref.at[pl.ds(s3 + s2, s2), pl.ds(o2, o1)]),
            (i1, pack_ref.at[pl.ds(s3 + s2, s1), pl.ds(o2 + o1, o1)]),
        ]
        copies = [pltpu.make_async_copy(x, y, sems.at[i]) for i, (x, y) in enumerate(moves)]
        for copy in copies:
            copy.start()
        copies[0].wait()
        moved = moved_rows(tgt_ref[...], sizes, (CHIPS * part, s3 + s2, s3, 0))
        picks = [scatter_matrix(moved, part, part * (in_plane() ^ k)) for k in range(CHIPS)]
        picks.append(scatter_matrix(moved, s0, CHIPS * part))
        for i in range(count):
            rows = pl.ds(i * BLOCK, BLOCK)
            cols = pl.ds(0, (i + 1) * BLOCK)
            copies[3 * i + 1].wait()
            copies[3 * i + 2].wait()
            half = bf16(dot(inv[rows, cols], src[cols, :]))
            half_ref[rows, :] = half
            copies[3 * i + 3].wait()
            term = dot(cpl[:, rows], half)
            if i == 0:
                edge_ref[...] = term
            else:
                edge_ref[...] += term
        edge = bf16(edge_ref[...])
        lowest = bf16(dot(picks[CHIPS], edge))
        for pick, share in zip(picks, (share0, share1, share2, share3)):
            share[pl.ds(0, part), :] = bf16(dot(pick, edge))
            share[pl.ds(part, s0), :] = lowest
        for copy in copies[leaf:]:
            copy.wait()
        pack_ref[pl.ds(2 * s3, s0), pl.ds(0, o0)] = small0[...]
        pack_ref[pl.ds(s3 + s2 + s1, s1), pl.ds(o2 + o1, o0)] = small1[...]

    return call(
        kernel,
        "leaf_forward",
        (
            struct((inner, shots)),
            *[struct((part + s0, shots))] * CHIPS,
            struct((2 * s3 + s0, o3)),
        ),
        (src, inv, cpl, tgt, *separators, *parents),
        [HBM] * 11,
        (VMEM,) * (CHIPS + 2),
        600_000_000,
        scratch=[
            pltpu.VMEM(src.shape, jnp.bfloat16),
            pltpu.VMEM(inv.shape, jnp.bfloat16),
            pltpu.VMEM(cpl.shape, jnp.bfloat16),
            pltpu.VMEM((cpl.shape[0], shots), jnp.float32),
            pltpu.VMEM((s0, o0), jnp.bfloat16),
            pltpu.VMEM((s1, o0), jnp.bfloat16),
            pltpu.VMEM(tgt.shape, jnp.int32),
            pltpu.SemaphoreType.DMA((3 * count + 8,)),
        ],
    )


def share_rows(sizes):
    return sum(sizes[1:]) // CHIPS, sizes[1] // CHIPS


def ordered(first, own, other):
    return jnp.concatenate([jnp.where(first, own, other), jnp.where(first, other, own)], 0)


def plane_sum(pieces, pack, far_pack, separators, parents):
    sizes = [m.shape[0] for m in separators]
    s0, s1, s2, s3 = sizes
    o0, o1, o2, _ = [m.shape[1] for m in separators]
    part, side = share_rows(sizes)
    shots = pieces[0].shape[1]

    def kernel(a, b, c, d, pack_ref, far_pack_ref, share_ref, low_ref):
        first = lax.axis_index("sep") == 0
        total = sum(x[...].astype(jnp.float32) for x in (a, b, c, d))
        low = bf16(total[part:])
        low_ref[...] = low
        share_ref[pl.ds(0, part - s1), :] = bf16(total[: part - s1])
        inv_at = (pl.ds(2 * s3, s0), pl.ds(0, o0))
        cpl_at = (pl.ds(s3 + s2 + s1, s1), pl.ds(o2 + o1, o0))
        inv = ordered(first, pack_ref[inv_at], far_pack_ref[inv_at])
        up = bf16(dot(inv, ordered(first, low, jnp.zeros_like(low))))
        own, far = dot(pack_ref[cpl_at], up), dot(far_pack_ref[cpl_at], up)
        me = in_plane()
        end = total[part - s1 : part] + jnp.where(me == CHIPS - 1, own, 0.0)
        share_ref[pl.ds(part - s1, s1), :] = bf16(end)
        kept = far[:side]
        for q in range(1, CHIPS):
            kept = jnp.where(me == q, far[q * side : (q + 1) * side], kept)
        share_ref[pl.ds(part, side), :] = bf16(kept)

    return call(
        kernel,
        "plane_sum",
        (struct((part + side, shots)), struct((s0, shots))),
        (*pieces, pack, far_pack),
        [VMEM] * 6,
        (VMEM, VMEM),
        10_000_000,
        limit=4,
    )


def exchange_columns(cols):
    i = lax.broadcasted_iota(jnp.int32, (cols, cols), 0)
    j = lax.broadcasted_iota(jnp.int32, (cols, cols), 1)
    return bf16(jnp.where((i - j == cols // 2) | (j - i == cols // 2), 1.0, 0.0))


def solve_operator(pack, far_pack, lift, separators, parents):
    s = [m.shape[0] for m in separators]
    o = [m.shape[1] for m in separators]
    total = sum(s)
    inner = lift.shape[0]
    width = sum(s) + s[1]

    def kernel(own_ref, far_ref, lift_ref, out_ref, far_out_ref):
        first = lax.axis_index("sep") == 0

        def whole(row, rows, col, cols):
            at = (pl.ds(row, rows), pl.ds(col, cols))
            return ordered(first, own_ref[at], far_ref[at])

        def own_columns(x):
            half = x.shape[1] // 2
            if half % 128:
                return jnp.where(first, x, bf16(dot(x, exchange_columns(2 * half))))
            return jnp.where(first, x, jnp.concatenate([x[:, half:], x[:, :half]], 1))

        x3 = own_columns(whole(0, s[3], 0, o[3]))
        c2 = whole(s[3], s[3], 0, o[2])
        x2 = whole(s[3], s[2], o[2], o[2])
        c1 = whole(s[3] + s[2], s[2], o[2], o[1])
        x1 = whole(s[3] + s[2], s[1], o[2] + o[1], o[1])
        c0 = whole(s[3] + s[2] + s[1], s[1], o[2] + o[1], o[0])
        x0 = own_columns(whole(2 * s[3], s[0], 0, o[0]))
        t3 = bf16(dot(whole(0, s[3], 0, o[3]), c2))
        t2 = bf16(dot(x2, c1))
        t1 = bf16(dot(x1, c0))
        x2, x1 = own_columns(x2), own_columns(x1)
        n32 = bf16(dot(t3, x2))
        n21 = bf16(dot(t2, x1))
        n10 = bf16(dot(t1, x0))
        n31 = bf16(dot(t3, n21))
        n20 = bf16(dot(t2, n10))
        n30 = bf16(dot(t3, n20))

        def turned(x, sign):
            y = x.astype(jnp.float32).T
            return bf16(sign * y[: y.shape[0] // 2])

        m3 = jnp.concatenate([turned(x3, 1.0), turned(n32, -1.0), turned(n31, 1.0), turned(n30, -1.0)], 0)
        m2 = jnp.concatenate([turned(x2, 1.0), turned(n21, -1.0), turned(n20, 1.0)], 0)
        m1 = jnp.concatenate([turned(x1, 1.0), turned(n10, -1.0)], 0)
        m0 = turned(x0, 1.0)
        top, mid, low = s[3], s[3] + s[2], s[3] + s[2] + s[1]
        a3 = bf16(dot(m3, x3))
        out_ref[pl.ds(0, total), pl.ds(0, top)] = a3[:, :top]
        far_out_ref[pl.ds(0, total), pl.ds(0, top)] = a3[:, top:]
        a2 = dot(m3, n32)
        a2 = bf16(jnp.concatenate([a2[:top], a2[top:] + dot(m2, x2)], 0))
        out_ref[pl.ds(0, total), pl.ds(top, s[2])] = a2[:, : s[2]]
        far_out_ref[pl.ds(0, total), pl.ds(top, s[2])] = a2[:, s[2] :]
        a1 = dot(m3, n31)
        rest = a1[top:] + dot(m2, n21)
        a1 = bf16(jnp.concatenate([a1[:top], rest[: s[2]], rest[s[2] :] + dot(m1, x1)], 0))
        out_ref[pl.ds(0, total), pl.ds(mid, o[1])] = a1
        far_out_ref[pl.ds(0, total), pl.ds(mid, o[1])] = bf16(dot(a1, exchange_columns(o[1])))
        a0 = bf16(dot(m0, x0))
        for ref, block in ((out_ref, a0), (far_out_ref, bf16(dot(a0, exchange_columns(o[0]))))):
            ref[pl.ds(0, low), pl.ds(mid + o[1], s[0])] = jnp.zeros((low, s[0]), jnp.bfloat16)
            ref[pl.ds(low, s[0]), pl.ds(mid + o[1], s[0])] = block[:, : s[0]]
            ref[pl.ds(total, inner), :] = bf16(-dot(lift_ref[...], ref[pl.ds(0, total), :]))

    shape = struct((total + inner, width))
    return call(
        kernel,
        "solve_operator",
        (shape, shape),
        (pack, far_pack, lift),
        [VMEM] * 3,
        (VMEM, VMEM),
        2_000_000_000,
    )


def leaf_backward(inv, cpl, tgt, half, sizes):
    inner, shots = half.shape
    count = inner // BLOCK
    total = sum(sizes)

    def kernel(inv_ref, cpl_ref, tgt_ref, half_ref, direct_ref, lift_ref, reach_ref):
        onehot = scatter_matrix(moved_rows(tgt_ref[...], sizes, places(sizes)), total)
        for i in range(count):
            cols = pl.ds(i * BLOCK, BLOCK)
            reach_ref[:, cols] = bf16(dot(onehot, cpl_ref[:, cols]))
        for j in range(count):
            rows = pl.ds(j * BLOCK, inner - j * BLOCK)
            cols = pl.ds(j * BLOCK, BLOCK)
            block = inv_ref[rows, cols]
            direct_ref[cols, :] = dot_tn(block, half_ref[rows, :])
            lift_ref[cols, :] = bf16(dot(reach_ref[:, rows], block).T)

    return call(
        kernel,
        "leaf_backward",
        (struct((inner, shots), jnp.float32), struct((inner, total))),
        (inv, cpl, tgt, half),
        [VMEM] * 4,
        (VMEM, VMEM),
        1_000_000_000,
        scratch=[pltpu.VMEM((total, inner), jnp.bfloat16)],
    )


def collect(rows, shared_ref, sizes):
    part, side = share_rows(sizes)
    each = part + side
    for q in range(CHIPS):
        at = pl.multiple_of((in_plane() ^ q) * each, each)
        rows[pl.ds(q * part, part), :] = shared_ref[pl.ds(at, part), :]
        rows[pl.ds(CHIPS * part + q * side, side), :] = shared_ref[pl.ds(at + part, side), :]


def own_part(shared, low, far_low, solve, far_solve, direct, sizes):
    total, s0 = sum(sizes), sizes[0]
    inner, shots = direct.shape
    height, width = solve.shape
    upper = width - s0

    def kernel(shared_ref, low_ref, far_low_ref, solve_ref, far_ref, direct_ref, out_ref, rhs):
        collect(rhs, shared_ref, sizes)
        rhs[pl.ds(upper, s0), :] = low_ref[...]
        sum_ = dot(solve_ref[...], rhs[...]) + dot(far_ref[:, pl.ds(upper, s0)], far_low_ref[...])
        out_ref[pl.ds(0, total), :] = sum_[:total]
        out_ref[pl.ds(total, inner), :] = sum_[total:] + direct_ref[...]

    return call(
        kernel,
        "own_part",
        struct((height, shots), jnp.float32),
        (shared, low, far_low, solve, far_solve, direct),
        [VMEM] * 6,
        VMEM,
        400_000_000,
        scratch=[pltpu.VMEM((width, shots), jnp.bfloat16)],
    )


def finish(shared, solve, own, sizes):
    total = sum(sizes)
    shots = shared.shape[1]
    upper = shared.shape[0]
    inner = own.shape[0] - total
    count = inner // BLOCK

    def kernel(shared_ref, solve_ref, own_ref, inner_hbm, sep_hbm, rhs, inner_buf, sep_buf, sems):
        collect(rhs, shared_ref, sizes)

        def block(start, size):
            rows = pl.ds(start, size)
            return bf16(own_ref[rows, :] + dot(solve_ref[rows, pl.ds(0, upper)], rhs[...]))

        down = block(0, total)
        for begin, place, size in zip(offsets(sizes), places(sizes), sizes):
            sep_buf[pl.ds(begin, size), :] = down[place : place + size]
        copies = [pltpu.make_async_copy(sep_buf, sep_hbm, sems.at[count])]
        copies[0].start()
        for i in range(count):
            rows = pl.ds(i * BLOCK, BLOCK)
            inner_buf[rows, :] = block(total + i * BLOCK, BLOCK)
            copies.append(pltpu.make_async_copy(inner_buf.at[rows], inner_hbm.at[rows], sems.at[i]))
            copies[-1].start()
        for copy in copies:
            copy.wait()

    return call(
        kernel,
        "finish",
        (struct((inner, shots)), struct((total, shots))),
        (shared, solve, own),
        [VMEM] * 3,
        (HBM, HBM),
        400_000_000,
        scratch=[
            pltpu.VMEM((upper, shots), jnp.bfloat16),
            pltpu.VMEM((inner, shots), jnp.bfloat16),
            pltpu.VMEM((total, shots), jnp.bfloat16),
            pltpu.SemaphoreType.DMA((count + 1,)),
        ],
    )


def other_strip(x):
    return lax.ppermute(x, "sep", [(0, 1), (1, 0)])


def partner(x, mask):
    return lax.ppermute(x, "sub", [(s, s ^ mask) for s in range(lax.axis_size("sub"))])


def added(*terms):
    return bf16(sum(t.astype(jnp.float32) for t in terms))


def local(sources, inner_inv, coupling, boundary_map, *blocks):
    src, inv, cpl, tgt = sources[0, 0], inner_inv[0, 0], coupling[0, 0], boundary_map[0]
    separators = [m[0] for m in blocks[:4]]
    parents = [m[0] for m in blocks[4:]]
    sizes = [m.shape[0] for m in separators]
    half, *parts, pack = leaf_forward(src, inv, cpl, tgt, separators, parents)
    pieces = parts[:1] + [partner(parts[k], k) for k in range(1, CHIPS)]
    direct, lift = leaf_backward(inv, cpl, tgt, half, sizes)
    far_pack = other_strip(pack)
    share, low = plane_sum(pieces, pack, far_pack, separators, parents)
    far_low = other_strip(low)
    solve, far_solve = solve_operator(pack, far_pack, lift, separators, parents)
    along = [partner(share, CHIPS * k) for k in range(1, CHIPS)]
    along, far_low, direct, solve, far_solve = lax.optimization_barrier((along, far_low, direct, solve, far_solve))
    share = added(share, *along)
    shared = jnp.concatenate([share] + [partner(share, k) for k in range(1, CHIPS)], 0)
    own = own_part(shared, low, far_low, solve, far_solve, direct, sizes)
    inner, sep = finish(other_strip(shared), far_solve, own, sizes)
    return (inner[None, None], sep[None, None])


def local_any(sources, inner_inv, coupling, boundary_map, *blocks):
    src, inv, cpl, tgt = sources[0, 0], inner_inv[0, 0], coupling[0, 0], boundary_map[0, 0]
    separators = [m[0] for m in blocks[:4]]
    parents = [m[0] for m in blocks[4:]]
    sizes = [m.shape[0] for m in separators]
    levels = len(sizes)
    bits = lax.axis_size("sub").bit_length() - 1

    def both(x):
        return lax.all_gather(x, "sep", axis=0, tiled=True)

    half = bf16(dot(inv, src))
    edge = bf16(dot(cpl, half))
    slots = lax.broadcasted_iota(jnp.int32, (sum(sizes), tgt.shape[0]), 0)
    carried = dot(bf16(slots == tgt[None, :]), edge)
    ups = []
    for level, size in enumerate(sizes):
        for bit in range(2 * level, min(2 * level + 2, bits)):
            sent = partner(bf16(carried), 1 << bit)
            carried = carried + sent.astype(jnp.float32)
        up = both(bf16(dot(separators[level], both(bf16(carried[:size])))))
        ups.append(up)
        carried = carried[size:]
        if level < levels - 1:
            carried = carried.at[: sizes[level + 1]].add(dot(parents[level], up))
    own, down = [None] * levels, None
    for level in reversed(range(levels)):
        target = ups[level]
        if down is not None:
            target = bf16(target.astype(jnp.float32) - dot_tn(both(parents[level]), down))
        down = bf16(dot_tn(both(separators[level]), target))
        own[level] = lax.dynamic_slice_in_dim(down, lax.axis_index("sep") * sizes[level], sizes[level], 0)
    sep = jnp.concatenate(own, 0)
    lifted = bf16(dot_tn(cpl, jnp.take(sep, tgt, axis=0)))
    inner = bf16(dot_tn(inv, half) - dot_tn(inv, lifted))
    return (inner[None, None], sep[None, None])


def solution(mesh):
    whole = P("sub", "sep", None, None)
    placed = (whole,) * 2 + (whole, P("sub", "sep", None)) + (P("sub", "sep", None),) * 7
    two_stages = mesh.shape["sub"] == CHIPS * CHIPS
    return jax.shard_map(
        local if two_stages else local_any,
        mesh=mesh,
        in_specs=placed,
        out_specs=(whole, whole),
        check_vma=False,
    )
```

```python
import jax
import jax.numpy as jnp
from jax import lax
from jax.experimental import pallas as pl
from jax.experimental.pallas import tpu as pltpu
from jax.sharding import PartitionSpec as P

BLOCK = 256
CHIPS = 4
IN_PLANE = (3, 1, 2)
ALONG = (1, 3, 2)
AROUND = ((2, False), (1, False), (3, True))
MIB = 1024 * 1024
VMEM = pl.BlockSpec(memory_space=pltpu.VMEM)
HBM = pl.BlockSpec(memory_space=pltpu.HBM)


def bf16(x):
    return x.astype(jnp.bfloat16)


def dot(a, b):
    return jnp.dot(a, b, preferred_element_type=jnp.float32)


def dot_tn(a, b):
    return lax.dot_general(a, b, (((0,), (0,)), ((), ())), preferred_element_type=jnp.float32)


def call(kernel, name, outs, ins, specs, out_specs, flops, limit=16, scratch=()):
    ins = [pltpu.with_memory_space_constraint(x, pltpu.HBM) if s is HBM else x for x, s in zip(ins, specs)]
    moved = sum(x.size * x.dtype.itemsize for x in ins)
    return pl.pallas_call(
        kernel,
        out_shape=outs,
        in_specs=specs,
        out_specs=out_specs,
        scratch_shapes=list(scratch),
        compiler_params=pltpu.CompilerParams(vmem_limit_bytes=limit * MIB),
        cost_estimate=pl.CostEstimate(flops=flops, bytes_accessed=moved, transcendentals=0),
        name=name,
    )(*ins)


def in_plane():
    return lax.rem(lax.axis_index("sub"), CHIPS)


def struct(shape, dtype=jnp.bfloat16):
    return jax.ShapeDtypeStruct(shape, dtype)


def offsets(sizes):
    return [sum(sizes[:i]) for i in range(len(sizes))]


def places(sizes):
    return [sum(sizes[i + 1 :]) for i in range(len(sizes))]


def moved_rows(tgt, sizes, order):
    moved = tgt
    for start, place, size in zip(offsets(sizes), order, sizes):
        inside = (tgt >= start) & (tgt < start + size)
        moved = jnp.where(inside, tgt + (place - start), moved)
    return moved


def scatter_matrix(moved, rows, start=0):
    slots = lax.broadcasted_iota(jnp.int32, (rows, moved.shape[1]), 0)
    return bf16(jnp.where(slots + start == moved, 1.0, 0.0))


def leaf_forward(src, inv, cpl, tgt, separators, parents):
    inner, shots = src.shape
    count = inner // BLOCK
    sizes = [m.shape[0] for m in separators]
    s0, s1, s2, s3 = sizes
    o0, o1, o2, o3 = [m.shape[1] for m in separators]
    part, _ = share_rows(sizes)

    def kernel(src_hbm, inv_hbm, cpl_hbm, tgt_hbm, i0, i1, i2, i3, c0, c1, c2,
               half_ref, share0, share1, share2, share3, pack_ref,
               src, inv, cpl, edge_ref, small0, small1, tgt_ref, sems):
        moves = [(tgt_hbm, tgt_ref)]
        for i in range(count):
            rows = pl.ds(i * BLOCK, BLOCK)
            cols = pl.ds(0, (i + 1) * BLOCK)
            moves.append((src_hbm.at[rows], src.at[rows]))
            moves.append((inv_hbm.at[rows, cols], inv.at[rows, cols]))
            moves.append((cpl_hbm.at[:, rows], cpl.at[:, rows]))
        leaf = len(moves)
        moves += [
            (i0, small0),
            (c0, small1),
            (i3, pack_ref.at[pl.ds(0, s3), :]),
            (c2, pack_ref.at[pl.ds(s3, s3), pl.ds(0, o2)]),
            (i2, pack_ref.at[pl.ds(s3, s2), pl.ds(o2, o2)]),
            (c1, pack_ref.at[pl.ds(s3 + s2, s2), pl.ds(o2, o1)]),
            (i1, pack_ref.at[pl.ds(s3 + s2, s1), pl.ds(o2 + o1, o1)]),
        ]
        copies = [pltpu.make_async_copy(x, y, sems.at[i]) for i, (x, y) in enumerate(moves)]
        for copy in copies:
            copy.start()
        copies[0].wait()
        moved = moved_rows(tgt_ref[...], sizes, (CHIPS * part, s3 + s2, s3, 0))
        picks = [scatter_matrix(moved, part, part * (in_plane() ^ k)) for k in range(CHIPS)]
        picks = jnp.concatenate([*picks, scatter_matrix(moved, s0, CHIPS * part)], 0)
        for i in range(count):
            rows = pl.ds(i * BLOCK, BLOCK)
            cols = pl.ds(0, (i + 1) * BLOCK)
            copies[3 * i + 1].wait()
            copies[3 * i + 2].wait()
            half = bf16(dot(inv[rows, cols], src[cols, :]))
            half_ref[rows, :] = half
            copies[3 * i + 3].wait()
            term = dot(cpl[:, rows], half)
            if i == 0:
                edge_ref[...] = term
            else:
                edge_ref[...] += term
        edge = bf16(edge_ref[...])
        out = bf16(dot(picks, edge))
        for k, share in enumerate((share0, share1, share2, share3)):
            share[pl.ds(0, part), :] = out[k * part : (k + 1) * part]
            share[pl.ds(part, s0), :] = out[CHIPS * part :]
        for copy in copies[leaf:]:
            copy.wait()
        pack_ref[pl.ds(2 * s3, s0), pl.ds(0, o0)] = small0[...]
        pack_ref[pl.ds(s3 + s2 + s1, s1), pl.ds(o2 + o1, o0)] = small1[...]

    return call(
        kernel,
        "leaf_forward",
        (
            struct((inner, shots)),
            *[struct((part + s0, shots))] * CHIPS,
            struct((2 * s3 + s0, o3)),
        ),
        (src, inv, cpl, tgt, *separators, *parents),
        [HBM] * 11,
        (VMEM,) * (CHIPS + 2),
        600_000_000,
        scratch=[
            pltpu.VMEM(src.shape, jnp.bfloat16),
            pltpu.VMEM(inv.shape, jnp.bfloat16),
            pltpu.VMEM(cpl.shape, jnp.bfloat16),
            pltpu.VMEM((cpl.shape[0], shots), jnp.float32),
            pltpu.VMEM((s0, o0), jnp.bfloat16),
            pltpu.VMEM((s1, o0), jnp.bfloat16),
            pltpu.VMEM(tgt.shape, jnp.int32),
            pltpu.SemaphoreType.DMA((3 * count + 8,)),
        ],
    )


def share_rows(sizes):
    return sum(sizes[1:]) // CHIPS, sizes[1] // CHIPS


def ordered(first, own, other):
    return jnp.concatenate([jnp.where(first, own, other), jnp.where(first, other, own)], 0)


def plane_sum(pieces, pack, far_pack, separators, parents):
    sizes = [m.shape[0] for m in separators]
    s0, s1, s2, s3 = sizes
    o0, o1, o2, _ = [m.shape[1] for m in separators]
    part, side = share_rows(sizes)
    shots = pieces[0].shape[1]

    def kernel(a, b, c, d, pack_ref, far_pack_ref, share_ref, low_ref):
        first = lax.axis_index("sep") == 0
        total = sum(x[...].astype(jnp.float32) for x in (a, b, c, d))
        low = bf16(total[part:])
        low_ref[...] = low
        share_ref[pl.ds(0, part - s1), :] = bf16(total[: part - s1])
        inv_at = (pl.ds(2 * s3, s0), pl.ds(0, o0))
        cpl_at = (pl.ds(s3 + s2 + s1, s1), pl.ds(o2 + o1, o0))
        inv = ordered(first, pack_ref[inv_at], far_pack_ref[inv_at])
        up = bf16(dot(inv, ordered(first, low, jnp.zeros_like(low))))
        own, far = dot(pack_ref[cpl_at], up), dot(far_pack_ref[cpl_at], up)
        me = in_plane()
        end = total[part - s1 : part] + jnp.where(me == CHIPS - 1, own, 0.0)
        share_ref[pl.ds(part - s1, s1), :] = bf16(end)
        kept = far[:side]
        for q in range(1, CHIPS):
            kept = jnp.where(me == q, far[q * side : (q + 1) * side], kept)
        share_ref[pl.ds(part, side), :] = bf16(kept)

    return call(
        kernel,
        "plane_sum",
        (struct((part + side, shots)), struct((s0, shots))),
        (*pieces, pack, far_pack),
        [VMEM] * 6,
        (VMEM, VMEM),
        10_000_000,
        limit=4,
    )


def exchange_columns(cols):
    i = lax.broadcasted_iota(jnp.int32, (cols, cols), 0)
    j = lax.broadcasted_iota(jnp.int32, (cols, cols), 1)
    return bf16(jnp.where((i - j == cols // 2) | (j - i == cols // 2), 1.0, 0.0))


def solve_operator(pack, far_pack, separators, parents):
    s = [m.shape[0] for m in separators]
    o = [m.shape[1] for m in separators]
    total = sum(s)
    part, side = share_rows(s)
    width = CHIPS * (part + side)

    def share_order():
        i = lax.broadcasted_iota(jnp.int32, (width, width), 0)
        j = lax.broadcasted_iota(jnp.int32, (width, width), 1)
        q, r = j // (part + side), j % (part + side)
        from_ = jnp.where(r < part, q * part + r, CHIPS * part + q * side + r - part)
        return bf16(jnp.where(i == from_, 1.0, 0.0))

    def kernel(own_ref, far_ref, out_ref, far_out_ref, low_ref, levels, far_levels):
        first = lax.axis_index("sep") == 0

        def whole(row, rows, col, cols):
            at = (pl.ds(row, rows), pl.ds(col, cols))
            return ordered(first, own_ref[at], far_ref[at])

        def own_columns(x):
            half = x.shape[1] // 2
            if half % 128:
                return jnp.where(first, x, bf16(dot(x, exchange_columns(2 * half))))
            return jnp.where(first, x, jnp.concatenate([x[:, half:], x[:, :half]], 1))

        x3 = own_columns(whole(0, s[3], 0, o[3]))
        c2 = whole(s[3], s[3], 0, o[2])
        x2 = whole(s[3], s[2], o[2], o[2])
        c1 = whole(s[3] + s[2], s[2], o[2], o[1])
        x1 = whole(s[3] + s[2], s[1], o[2] + o[1], o[1])
        c0 = whole(s[3] + s[2] + s[1], s[1], o[2] + o[1], o[0])
        x0 = own_columns(whole(2 * s[3], s[0], 0, o[0]))
        t3 = bf16(dot(whole(0, s[3], 0, o[3]), c2))
        t2 = bf16(dot(x2, c1))
        t1 = bf16(dot(x1, c0))
        x2, x1 = own_columns(x2), own_columns(x1)
        n32 = bf16(dot(t3, x2))
        n21 = bf16(dot(t2, x1))
        n10 = bf16(dot(t1, x0))
        n31 = bf16(dot(t3, n21))
        n20 = bf16(dot(t2, n10))
        n30 = bf16(dot(t3, n20))

        def turned(x, sign):
            y = x.astype(jnp.float32).T
            return bf16(sign * y[: y.shape[0] // 2])

        m3 = jnp.concatenate([turned(x3, 1.0), turned(n32, -1.0), turned(n31, 1.0), turned(n30, -1.0)], 0)
        m2 = jnp.concatenate([turned(x2, 1.0), turned(n21, -1.0), turned(n20, 1.0)], 0)
        m1 = jnp.concatenate([turned(x1, 1.0), turned(n10, -1.0)], 0)
        m0 = turned(x0, 1.0)
        top, mid, low = s[3], s[3] + s[2], s[3] + s[2] + s[1]
        a3 = bf16(dot(m3, x3))
        levels[:, pl.ds(0, top)] = a3[:, :top]
        far_levels[:, pl.ds(0, top)] = a3[:, top:]
        a2 = dot(m3, n32)
        a2 = bf16(jnp.concatenate([a2[:top], a2[top:] + dot(m2, x2)], 0))
        levels[:, pl.ds(top, s[2])] = a2[:, : s[2]]
        far_levels[:, pl.ds(top, s[2])] = a2[:, s[2] :]
        a1 = dot(m3, n31)
        rest = a1[top:] + dot(m2, n21)
        a1 = bf16(jnp.concatenate([a1[:top], rest[: s[2]], rest[s[2] :] + dot(m1, x1)], 0))
        levels[:, pl.ds(mid, o[1])] = a1
        far_levels[:, pl.ds(mid, o[1])] = bf16(dot(a1, exchange_columns(o[1])))
        order = share_order()
        out_ref[...] = bf16(dot(levels[...], order))
        far_out_ref[...] = bf16(dot(far_levels[...], order))
        low_ref[pl.ds(0, low), :] = jnp.zeros((low, o[0]), jnp.bfloat16)
        low_ref[pl.ds(low, s[0]), :] = bf16(dot(m0, x0))

    shape = struct((total, width))
    return call(
        kernel,
        "solve_operator",
        (shape, shape, struct((total, o[0]))),
        (pack, far_pack),
        [VMEM] * 2,
        (VMEM,) * 3,
        1_000_000_000,
        scratch=[pltpu.VMEM((total, width), jnp.bfloat16)] * 2,
    )


def correction_operator(solve, far_solve, low_solve, lift, sizes):
    total, width = solve.shape
    inner = lift.shape[0]
    each = sum(share_rows(sizes))

    def kernel(solve_ref, far_ref, low_solve_ref, lift_ref, held_ref, other_ref, low_ref):
        for i, (mask, own) in enumerate(((0, True), *AROUND)):
            cols = pl.ds(i * each, each)
            at = pl.ds(pl.multiple_of((in_plane() ^ mask) * each, each), each)
            held_ref[pl.ds(0, total), cols] = (solve_ref if own else far_ref)[:, at]
            other_ref[pl.ds(0, total), cols] = (far_ref if own else solve_ref)[:, at]
        low_ref[pl.ds(0, total), :] = low_solve_ref[...]
        for ref in (held_ref, other_ref, low_ref):
            ref[pl.ds(total, inner), :] = bf16(-dot(lift_ref[...], ref[pl.ds(0, total), :]))

    shape = struct((total + inner, width))
    return call(
        kernel,
        "correction_operator",
        (shape, shape, struct((total + inner, low_solve.shape[1]))),
        (solve, far_solve, low_solve, lift),
        [VMEM] * 4,
        (VMEM,) * 3,
        1_000_000_000,
    )


def leaf_backward(inv, cpl, tgt, half, sizes):
    inner, shots = half.shape
    count = inner // BLOCK
    total = sum(sizes)

    def kernel(inv_ref, cpl_ref, tgt_ref, half_ref, direct_ref, lift_ref, reach_ref):
        onehot = scatter_matrix(moved_rows(tgt_ref[...], sizes, places(sizes)), total)
        for i in range(count):
            cols = pl.ds(i * BLOCK, BLOCK)
            reach_ref[:, cols] = bf16(dot(onehot, cpl_ref[:, cols]))
        for j in range(count):
            rows = pl.ds(j * BLOCK, inner - j * BLOCK)
            cols = pl.ds(j * BLOCK, BLOCK)
            block = inv_ref[rows, cols]
            direct_ref[cols, :] = dot_tn(block, half_ref[rows, :])
            lift_ref[cols, :] = bf16(dot(reach_ref[:, rows], block).T)

    return call(
        kernel,
        "leaf_backward",
        (struct((inner, shots), jnp.float32), struct((inner, total))),
        (inv, cpl, tgt, half),
        [VMEM] * 4,
        (VMEM, VMEM),
        1_000_000_000,
        scratch=[pltpu.VMEM((total, inner), jnp.bfloat16)],
    )


def own_part(held, low, far_low, operator, low_operator, direct, sizes):
    total = sum(sizes)
    inner, shots = direct.shape

    def kernel(held_ref, low_ref, far_low_ref, operator_ref, low_operator_ref, direct_ref, out_ref):
        low = jnp.concatenate([low_ref[...], far_low_ref[...]], 0)
        out = dot(operator_ref[...], held_ref[...]) + dot(low_operator_ref[...], low)
        out_ref[pl.ds(0, total), :] = out[:total]
        out_ref[pl.ds(total, inner), :] = out[total:] + direct_ref[...]

    return call(
        kernel,
        "own_part",
        struct((total + inner, shots), jnp.float32),
        (held, low, far_low, operator, low_operator, direct),
        [VMEM] * 6,
        VMEM,
        400_000_000,
    )


def finish(held, operator, own, sizes):
    total = sum(sizes)
    shots = held.shape[1]
    inner = own.shape[0] - total
    count = inner // BLOCK

    def kernel(held_ref, operator_ref, own_ref, inner_hbm, sep_hbm, inner_buf, sep_buf, sems):
        def block(start, size):
            rows = pl.ds(start, size)
            return bf16(own_ref[rows, :] + dot(operator_ref[rows, :], held_ref[...]))

        down = block(0, total)
        for begin, place, size in zip(offsets(sizes), places(sizes), sizes):
            sep_buf[pl.ds(begin, size), :] = down[place : place + size]
        copies = [pltpu.make_async_copy(sep_buf, sep_hbm, sems.at[count])]
        copies[0].start()
        for i in range(count):
            rows = pl.ds(i * BLOCK, BLOCK)
            inner_buf[rows, :] = block(total + i * BLOCK, BLOCK)
            copies.append(pltpu.make_async_copy(inner_buf.at[rows], inner_hbm.at[rows], sems.at[i]))
            copies[-1].start()
        for copy in copies:
            copy.wait()

    return call(
        kernel,
        "finish",
        (struct((inner, shots)), struct((total, shots))),
        (held, operator, own),
        [VMEM] * 3,
        (HBM, HBM),
        400_000_000,
        scratch=[
            pltpu.VMEM((inner, shots), jnp.bfloat16),
            pltpu.VMEM((total, shots), jnp.bfloat16),
            pltpu.SemaphoreType.DMA((count + 1,)),
        ],
    )


def other_strip(x):
    return lax.ppermute(x, "sep", [(0, 1), (1, 0)])


def partner(x, mask):
    return lax.ppermute(x, "sub", [(s, s ^ mask) for s in range(lax.axis_size("sub"))])


def partner_strip(x, mask):
    route = []
    for s in range(lax.axis_size("sub")):
        route += [(2 * s, 2 * (s ^ mask) + 1), (2 * s + 1, 2 * (s ^ mask))]
    return lax.ppermute(x, ("sub", "sep"), route)


def added(*terms):
    return bf16(sum(t.astype(jnp.float32) for t in terms))


def local(sources, inner_inv, coupling, boundary_map, *blocks):
    src, inv, cpl, tgt = sources[0, 0], inner_inv[0, 0], coupling[0, 0], boundary_map[0]
    separators = [m[0] for m in blocks[:4]]
    parents = [m[0] for m in blocks[4:]]
    sizes = [m.shape[0] for m in separators]
    half, *parts, pack = leaf_forward(src, inv, cpl, tgt, separators, parents)
    pieces = parts[:1] + [partner(parts[k], k) for k in IN_PLANE]
    direct, lift = leaf_backward(inv, cpl, tgt, half, sizes)
    far_pack = other_strip(pack)
    share, low = plane_sum(pieces, pack, far_pack, separators, parents)
    far_low = other_strip(low)
    solve = solve_operator(pack, far_pack, separators, parents)
    along = [partner(share, CHIPS * k) for k in ALONG]
    along, far_low, direct, lift, solve = lax.optimization_barrier((along, far_low, direct, lift, solve))
    share = added(share, *along)
    operators = correction_operator(*solve, lift, sizes)
    around = [partner(share, mask) if own else partner_strip(share, mask) for mask, own in AROUND]
    around, operators = lax.optimization_barrier((around, operators))
    held_operator, other_operator, low_operator = operators
    held = jnp.concatenate([share, *around], 0)
    own = own_part(held, low, far_low, held_operator, low_operator, direct, sizes)
    inner, sep = finish(other_strip(held), other_operator, own, sizes)
    return (inner[None, None], sep[None, None])


def local_any(sources, inner_inv, coupling, boundary_map, *blocks):
    src, inv, cpl, tgt = sources[0, 0], inner_inv[0, 0], coupling[0, 0], boundary_map[0, 0]
    separators = [m[0] for m in blocks[:4]]
    parents = [m[0] for m in blocks[4:]]
    sizes = [m.shape[0] for m in separators]
    levels = len(sizes)
    bits = lax.axis_size("sub").bit_length() - 1

    def both(x):
        return lax.all_gather(x, "sep", axis=0, tiled=True)

    half = bf16(dot(inv, src))
    edge = bf16(dot(cpl, half))
    slots = lax.broadcasted_iota(jnp.int32, (sum(sizes), tgt.shape[0]), 0)
    carried = dot(bf16(slots == tgt[None, :]), edge)
    ups = []
    for level, size in enumerate(sizes):
        for bit in range(2 * level, min(2 * level + 2, bits)):
            sent = partner(bf16(carried), 1 << bit)
            carried = carried + sent.astype(jnp.float32)
        up = both(bf16(dot(separators[level], both(bf16(carried[:size])))))
        ups.append(up)
        carried = carried[size:]
        if level < levels - 1:
            carried = carried.at[: sizes[level + 1]].add(dot(parents[level], up))
    own, down = [None] * levels, None
    for level in reversed(range(levels)):
        target = ups[level]
        if down is not None:
            target = bf16(target.astype(jnp.float32) - dot_tn(both(parents[level]), down))
        down = bf16(dot_tn(both(separators[level]), target))
        own[level] = lax.dynamic_slice_in_dim(down, lax.axis_index("sep") * sizes[level], sizes[level], 0)
    sep = jnp.concatenate(own, 0)
    lifted = bf16(dot_tn(cpl, jnp.take(sep, tgt, axis=0)))
    inner = bf16(dot_tn(inv, half) - dot_tn(inv, lifted))
    return (inner[None, None], sep[None, None])


def solution(mesh):
    whole = P("sub", "sep", None, None)
    placed = (whole,) * 2 + (whole, P("sub", "sep", None)) + (P("sub", "sep", None),) * 7
    two_stages = mesh.shape["sub"] == CHIPS * CHIPS
    return jax.shard_map(
        local if two_stages else local_any,
        mesh=mesh,
        in_specs=placed,
        out_specs=(whole, whole),
        check_vma=False,
    )
```

```python
import jax
import jax.numpy as jnp
from jax import lax
from jax.experimental import pallas as pl
from jax.experimental.pallas import tpu as pltpu
from jax.sharding import PartitionSpec as P

BLOCK = 256
CHIPS = 4
IN_PLANE = (3, 2, 1)
ALONG = (3, 2, 1)
AROUND = ((2, False), (1, False), (3, True))
MIB = 1024 * 1024
VMEM = pl.BlockSpec(memory_space=pltpu.VMEM)
HBM = pl.BlockSpec(memory_space=pltpu.HBM)


def bf16(x):
    return x.astype(jnp.bfloat16)


def dot(a, b):
    return jnp.dot(a, b, preferred_element_type=jnp.float32)


def dot_tn(a, b):
    return lax.dot_general(a, b, (((0,), (0,)), ((), ())), preferred_element_type=jnp.float32)


def call(kernel, name, outs, ins, specs, out_specs, flops, limit=16, scratch=()):
    ins = [pltpu.with_memory_space_constraint(x, pltpu.HBM) if s is HBM else x for x, s in zip(ins, specs)]
    moved = sum(x.size * x.dtype.itemsize for x in ins)
    return pl.pallas_call(
        kernel,
        out_shape=outs,
        in_specs=specs,
        out_specs=out_specs,
        scratch_shapes=list(scratch),
        compiler_params=pltpu.CompilerParams(vmem_limit_bytes=limit * MIB),
        cost_estimate=pl.CostEstimate(flops=flops, bytes_accessed=moved, transcendentals=0),
        name=name,
    )(*ins)


def in_plane():
    return lax.rem(lax.axis_index("sub"), CHIPS)


def struct(shape, dtype=jnp.bfloat16):
    return jax.ShapeDtypeStruct(shape, dtype)


def offsets(sizes):
    return [sum(sizes[:i]) for i in range(len(sizes))]


def places(sizes):
    return [sum(sizes[i + 1 :]) for i in range(len(sizes))]


def moved_rows(tgt, sizes, order):
    moved = tgt
    for start, place, size in zip(offsets(sizes), order, sizes):
        inside = (tgt >= start) & (tgt < start + size)
        moved = jnp.where(inside, tgt + (place - start), moved)
    return moved


def scatter_matrix(moved, rows, start=0):
    slots = lax.broadcasted_iota(jnp.int32, (rows, moved.shape[1]), 0)
    return bf16(jnp.where(slots + start == moved, 1.0, 0.0))


def leaf_forward(src, inv, cpl, tgt, separators, parents):
    inner, shots = src.shape
    count = inner // BLOCK
    sizes = [m.shape[0] for m in separators]
    s0, s1, s2, s3 = sizes
    o0, o1, o2, o3 = [m.shape[1] for m in separators]
    part, _ = share_rows(sizes)

    def kernel(src_hbm, inv_hbm, cpl_hbm, tgt_hbm, i0, i1, i2, i3, c0, c1, c2,
               half_ref, share0, share1, share2, share3, pack_ref,
               src, inv, cpl, edge_ref, small0, small1, tgt_ref, sems):
        moves = [(tgt_hbm, tgt_ref)]
        for i in range(count):
            rows = pl.ds(i * BLOCK, BLOCK)
            cols = pl.ds(0, (i + 1) * BLOCK)
            moves.append((src_hbm.at[rows], src.at[rows]))
            moves.append((inv_hbm.at[rows, cols], inv.at[rows, cols]))
            moves.append((cpl_hbm.at[:, rows], cpl.at[:, rows]))
        leaf = len(moves)
        moves += [
            (i0, small0),
            (c0, small1),
            (i3, pack_ref.at[pl.ds(0, s3), :]),
            (c2, pack_ref.at[pl.ds(s3, s3), pl.ds(0, o2)]),
            (i2, pack_ref.at[pl.ds(s3, s2), pl.ds(o2, o2)]),
            (c1, pack_ref.at[pl.ds(s3 + s2, s2), pl.ds(o2, o1)]),
            (i1, pack_ref.at[pl.ds(s3 + s2, s1), pl.ds(o2 + o1, o1)]),
        ]
        copies = [pltpu.make_async_copy(x, y, sems.at[i]) for i, (x, y) in enumerate(moves)]
        for copy in copies:
            copy.start()
        copies[0].wait()
        moved = moved_rows(tgt_ref[...], sizes, (CHIPS * part, s3 + s2, s3, 0))
        picks = [scatter_matrix(moved, part, part * (in_plane() ^ k)) for k in range(CHIPS)]
        picks = jnp.concatenate([*picks, scatter_matrix(moved, s0, CHIPS * part)], 0)
        for i in range(count):
            rows = pl.ds(i * BLOCK, BLOCK)
            cols = pl.ds(0, (i + 1) * BLOCK)
            copies[3 * i + 1].wait()
            copies[3 * i + 2].wait()
            half = bf16(dot(inv[rows, cols], src[cols, :]))
            half_ref[rows, :] = half
            copies[3 * i + 3].wait()
            term = dot(cpl[:, rows], half)
            if i == 0:
                edge_ref[...] = term
            else:
                edge_ref[...] += term
        edge = bf16(edge_ref[...])
        out = bf16(dot(picks, edge))
        for k, share in enumerate((share0, share1, share2, share3)):
            share[pl.ds(0, part), :] = out[k * part : (k + 1) * part]
            share[pl.ds(part, s0), :] = out[CHIPS * part :]
        for copy in copies[leaf:]:
            copy.wait()
        pack_ref[pl.ds(2 * s3, s0), pl.ds(0, o0)] = small0[...]
        pack_ref[pl.ds(s3 + s2 + s1, s1), pl.ds(o2 + o1, o0)] = small1[...]

    return call(
        kernel,
        "leaf_forward",
        (
            struct((inner, shots)),
            *[struct((part + s0, shots))] * CHIPS,
            struct((2 * s3 + s0, o3)),
        ),
        (src, inv, cpl, tgt, *separators, *parents),
        [HBM] * 11,
        (VMEM,) * (CHIPS + 2),
        600_000_000,
        scratch=[
            pltpu.VMEM(src.shape, jnp.bfloat16),
            pltpu.VMEM(inv.shape, jnp.bfloat16),
            pltpu.VMEM(cpl.shape, jnp.bfloat16),
            pltpu.VMEM((cpl.shape[0], shots), jnp.float32),
            pltpu.VMEM((s0, o0), jnp.bfloat16),
            pltpu.VMEM((s1, o0), jnp.bfloat16),
            pltpu.VMEM(tgt.shape, jnp.int32),
            pltpu.SemaphoreType.DMA((3 * count + 8,)),
        ],
    )


def share_rows(sizes):
    return sum(sizes[1:]) // CHIPS, sizes[1] // CHIPS


def ordered(first, own, other):
    return jnp.concatenate([jnp.where(first, own, other), jnp.where(first, other, own)], 0)


def plane_sum(pieces, pack, far_pack, separators, parents):
    sizes = [m.shape[0] for m in separators]
    s0, s1, s2, s3 = sizes
    o0, o1, o2, _ = [m.shape[1] for m in separators]
    part, side = share_rows(sizes)
    shots = pieces[0].shape[1]

    def kernel(a, b, c, d, pack_ref, far_pack_ref, share_ref, low_ref):
        first = lax.axis_index("sep") == 0
        total = sum(x[...].astype(jnp.float32) for x in (a, b, c, d))
        low = bf16(total[part:])
        low_ref[...] = low
        share_ref[pl.ds(0, part - s1), :] = bf16(total[: part - s1])
        inv_at = (pl.ds(2 * s3, s0), pl.ds(0, o0))
        cpl_at = (pl.ds(s3 + s2 + s1, s1), pl.ds(o2 + o1, o0))
        inv = ordered(first, pack_ref[inv_at], far_pack_ref[inv_at])
        up = bf16(dot(inv, ordered(first, low, jnp.zeros_like(low))))
        own, far = dot(pack_ref[cpl_at], up), dot(far_pack_ref[cpl_at], up)
        me = in_plane()
        end = total[part - s1 : part] + jnp.where(me == CHIPS - 1, own, 0.0)
        share_ref[pl.ds(part - s1, s1), :] = bf16(end)
        kept = far[:side]
        for q in range(1, CHIPS):
            kept = jnp.where(me == q, far[q * side : (q + 1) * side], kept)
        share_ref[pl.ds(part, side), :] = bf16(kept)

    return call(
        kernel,
        "plane_sum",
        (struct((part + side, shots)), struct((s0, shots))),
        (*pieces, pack, far_pack),
        [VMEM] * 6,
        (VMEM, VMEM),
        10_000_000,
        limit=4,
    )


def exchange_columns(cols):
    i = lax.broadcasted_iota(jnp.int32, (cols, cols), 0)
    j = lax.broadcasted_iota(jnp.int32, (cols, cols), 1)
    return bf16(jnp.where((i - j == cols // 2) | (j - i == cols // 2), 1.0, 0.0))


def solve_operator(pack, far_pack, separators, parents):
    s = [m.shape[0] for m in separators]
    o = [m.shape[1] for m in separators]
    total = sum(s)
    part, side = share_rows(s)
    width = CHIPS * (part + side)

    def share_order():
        i = lax.broadcasted_iota(jnp.int32, (width, width), 0)
        j = lax.broadcasted_iota(jnp.int32, (width, width), 1)
        q, r = j // (part + side), j % (part + side)
        from_ = jnp.where(r < part, q * part + r, CHIPS * part + q * side + r - part)
        return bf16(jnp.where(i == from_, 1.0, 0.0))

    def kernel(own_ref, far_ref, out_ref, far_out_ref, low_ref, levels, far_levels):
        first = lax.axis_index("sep") == 0

        def whole(row, rows, col, cols):
            at = (pl.ds(row, rows), pl.ds(col, cols))
            return ordered(first, own_ref[at], far_ref[at])

        def own_columns(x):
            half = x.shape[1] // 2
            if half % 128:
                return jnp.where(first, x, bf16(dot(x, exchange_columns(2 * half))))
            return jnp.where(first, x, jnp.concatenate([x[:, half:], x[:, :half]], 1))

        x3 = own_columns(whole(0, s[3], 0, o[3]))
        c2 = whole(s[3], s[3], 0, o[2])
        x2 = whole(s[3], s[2], o[2], o[2])
        c1 = whole(s[3] + s[2], s[2], o[2], o[1])
        x1 = whole(s[3] + s[2], s[1], o[2] + o[1], o[1])
        c0 = whole(s[3] + s[2] + s[1], s[1], o[2] + o[1], o[0])
        x0 = own_columns(whole(2 * s[3], s[0], 0, o[0]))
        t3 = bf16(dot(whole(0, s[3], 0, o[3]), c2))
        t2 = bf16(dot(x2, c1))
        t1 = bf16(dot(x1, c0))
        x2, x1 = own_columns(x2), own_columns(x1)
        n32 = bf16(dot(t3, x2))
        n21 = bf16(dot(t2, x1))
        n10 = bf16(dot(t1, x0))
        n31 = bf16(dot(t3, n21))
        n20 = bf16(dot(t2, n10))
        n30 = bf16(dot(t3, n20))

        def turned(x, sign):
            y = x.astype(jnp.float32).T
            return bf16(sign * y[: y.shape[0] // 2])

        m3 = jnp.concatenate([turned(x3, 1.0), turned(n32, -1.0), turned(n31, 1.0), turned(n30, -1.0)], 0)
        m2 = jnp.concatenate([turned(x2, 1.0), turned(n21, -1.0), turned(n20, 1.0)], 0)
        m1 = jnp.concatenate([turned(x1, 1.0), turned(n10, -1.0)], 0)
        m0 = turned(x0, 1.0)
        top, mid, low = s[3], s[3] + s[2], s[3] + s[2] + s[1]
        a3 = bf16(dot(m3, x3))
        levels[:, pl.ds(0, top)] = a3[:, :top]
        far_levels[:, pl.ds(0, top)] = a3[:, top:]
        a2 = dot(m3, n32)
        a2 = bf16(jnp.concatenate([a2[:top], a2[top:] + dot(m2, x2)], 0))
        levels[:, pl.ds(top, s[2])] = a2[:, : s[2]]
        far_levels[:, pl.ds(top, s[2])] = a2[:, s[2] :]
        a1 = dot(m3, n31)
        rest = a1[top:] + dot(m2, n21)
        a1 = bf16(jnp.concatenate([a1[:top], rest[: s[2]], rest[s[2] :] + dot(m1, x1)], 0))
        levels[:, pl.ds(mid, o[1])] = a1
        far_levels[:, pl.ds(mid, o[1])] = bf16(dot(a1, exchange_columns(o[1])))
        order = share_order()
        out_ref[...] = bf16(dot(levels[...], order))
        far_out_ref[...] = bf16(dot(far_levels[...], order))
        low_ref[pl.ds(0, low), :] = jnp.zeros((low, o[0]), jnp.bfloat16)
        low_ref[pl.ds(low, s[0]), :] = bf16(dot(m0, x0))

    shape = struct((total, width))
    return call(
        kernel,
        "solve_operator",
        (shape, shape, struct((total, o[0]))),
        (pack, far_pack),
        [VMEM] * 2,
        (VMEM,) * 3,
        1_000_000_000,
        scratch=[pltpu.VMEM((total, width), jnp.bfloat16)] * 2,
    )


def correction_operator(solve, far_solve, low_solve, lift, sizes):
    total, width = solve.shape
    inner = lift.shape[0]
    each = sum(share_rows(sizes))

    def kernel(solve_ref, far_ref, low_solve_ref, lift_ref, held_ref, other_ref, low_ref):
        for i, (mask, own) in enumerate(((0, True), *AROUND)):
            cols = pl.ds(i * each, each)
            at = pl.ds(pl.multiple_of((in_plane() ^ mask) * each, each), each)
            held_ref[pl.ds(0, total), cols] = (solve_ref if own else far_ref)[:, at]
            other_ref[pl.ds(0, total), cols] = (far_ref if own else solve_ref)[:, at]
        low_ref[pl.ds(0, total), :] = low_solve_ref[...]
        for ref in (held_ref, other_ref, low_ref):
            ref[pl.ds(total, inner), :] = bf16(-dot(lift_ref[...], ref[pl.ds(0, total), :]))

    shape = struct((total + inner, width))
    return call(
        kernel,
        "correction_operator",
        (shape, shape, struct((total + inner, low_solve.shape[1]))),
        (solve, far_solve, low_solve, lift),
        [VMEM] * 4,
        (VMEM,) * 3,
        1_000_000_000,
    )


def leaf_backward(inv, cpl, tgt, half, sizes):
    inner, shots = half.shape
    count = inner // BLOCK
    total = sum(sizes)

    def kernel(inv_ref, cpl_ref, tgt_ref, half_ref, direct_ref, lift_ref, reach_ref):
        onehot = scatter_matrix(moved_rows(tgt_ref[...], sizes, places(sizes)), total)
        for i in range(count):
            cols = pl.ds(i * BLOCK, BLOCK)
            reach_ref[:, cols] = bf16(dot(onehot, cpl_ref[:, cols]))
        for j in range(count):
            rows = pl.ds(j * BLOCK, inner - j * BLOCK)
            cols = pl.ds(j * BLOCK, BLOCK)
            block = inv_ref[rows, cols]
            direct_ref[cols, :] = dot_tn(block, half_ref[rows, :])
            lift_ref[cols, :] = bf16(dot(reach_ref[:, rows], block).T)

    return call(
        kernel,
        "leaf_backward",
        (struct((inner, shots), jnp.float32), struct((inner, total))),
        (inv, cpl, tgt, half),
        [VMEM] * 4,
        (VMEM, VMEM),
        1_000_000_000,
        scratch=[pltpu.VMEM((total, inner), jnp.bfloat16)],
    )


def own_part(held, low, far_low, operator, low_operator, direct, sizes):
    total = sum(sizes)
    inner, shots = direct.shape

    def kernel(held_ref, low_ref, far_low_ref, operator_ref, low_operator_ref, direct_ref, out_ref):
        low = jnp.concatenate([low_ref[...], far_low_ref[...]], 0)
        out = dot(operator_ref[...], held_ref[...]) + dot(low_operator_ref[...], low)
        out_ref[pl.ds(0, total), :] = out[:total]
        out_ref[pl.ds(total, inner), :] = out[total:] + direct_ref[...]

    return call(
        kernel,
        "own_part",
        struct((total + inner, shots), jnp.float32),
        (held, low, far_low, operator, low_operator, direct),
        [VMEM] * 6,
        VMEM,
        400_000_000,
    )


def finish(held, operator, own, sizes):
    total = sum(sizes)
    shots = held.shape[1]
    inner = own.shape[0] - total
    count = inner // BLOCK

    def kernel(held_ref, operator_ref, own_ref, inner_hbm, sep_hbm, inner_buf, sep_buf, sems):
        def block(start, size):
            rows = pl.ds(start, size)
            return bf16(own_ref[rows, :] + dot(operator_ref[rows, :], held_ref[...]))

        down = block(0, total)
        for begin, place, size in zip(offsets(sizes), places(sizes), sizes):
            sep_buf[pl.ds(begin, size), :] = down[place : place + size]
        copies = [pltpu.make_async_copy(sep_buf, sep_hbm, sems.at[count])]
        copies[0].start()
        for i in range(count):
            rows = pl.ds(i * BLOCK, BLOCK)
            inner_buf[rows, :] = block(total + i * BLOCK, BLOCK)
            copies.append(pltpu.make_async_copy(inner_buf.at[rows], inner_hbm.at[rows], sems.at[i]))
            copies[-1].start()
        for copy in copies:
            copy.wait()

    return call(
        kernel,
        "finish",
        (struct((inner, shots)), struct((total, shots))),
        (held, operator, own),
        [VMEM] * 3,
        (HBM, HBM),
        400_000_000,
        scratch=[
            pltpu.VMEM((inner, shots), jnp.bfloat16),
            pltpu.VMEM((total, shots), jnp.bfloat16),
            pltpu.SemaphoreType.DMA((count + 1,)),
        ],
    )


def other_strip(x):
    return lax.ppermute(x, "sep", [(0, 1), (1, 0)])


def partner(x, mask):
    return lax.ppermute(x, "sub", [(s, s ^ mask) for s in range(lax.axis_size("sub"))])


def shifted(x, planes):
    count = lax.axis_size("sub")
    return lax.ppermute(x, "sub", [(s, (s + CHIPS * planes) % count) for s in range(count)])


def partner_strip(x, mask):
    route = []
    for s in range(lax.axis_size("sub")):
        route += [(2 * s, 2 * (s ^ mask) + 1), (2 * s + 1, 2 * (s ^ mask))]
    return lax.ppermute(x, ("sub", "sep"), route)


def added(*terms):
    return bf16(sum(t.astype(jnp.float32) for t in terms))


def local(sources, inner_inv, coupling, boundary_map, *blocks):
    src, inv, cpl, tgt = sources[0, 0], inner_inv[0, 0], coupling[0, 0], boundary_map[0]
    separators = [m[0] for m in blocks[:4]]
    parents = [m[0] for m in blocks[4:]]
    sizes = [m.shape[0] for m in separators]
    half, *parts, pack = leaf_forward(src, inv, cpl, tgt, separators, parents)
    pieces = parts[:1] + [partner(parts[k], k) for k in IN_PLANE]
    direct, lift = leaf_backward(inv, cpl, tgt, half, sizes)
    far_pack = other_strip(pack)
    solve = solve_operator(pack, far_pack, separators, parents)
    pieces, solve = lax.optimization_barrier((pieces, solve))
    share, low = plane_sum(pieces, pack, far_pack, separators, parents)
    far_low = other_strip(low)
    along = [shifted(share, k) for k in ALONG]
    along, far_low, direct, lift = lax.optimization_barrier((along, far_low, direct, lift))
    share = added(share, *along)
    operators = correction_operator(*solve, lift, sizes)
    around = [partner(share, mask) if own else partner_strip(share, mask) for mask, own in AROUND]
    around, operators = lax.optimization_barrier((around, operators))
    held_operator, other_operator, low_operator = operators
    held = jnp.concatenate([share, *around], 0)
    own = own_part(held, low, far_low, held_operator, low_operator, direct, sizes)
    inner, sep = finish(other_strip(held), other_operator, own, sizes)
    return (inner[None, None], sep[None, None])


def local_any(sources, inner_inv, coupling, boundary_map, *blocks):
    src, inv, cpl, tgt = sources[0, 0], inner_inv[0, 0], coupling[0, 0], boundary_map[0, 0]
    separators = [m[0] for m in blocks[:4]]
    parents = [m[0] for m in blocks[4:]]
    sizes = [m.shape[0] for m in separators]
    levels = len(sizes)
    bits = lax.axis_size("sub").bit_length() - 1

    def both(x):
        return lax.all_gather(x, "sep", axis=0, tiled=True)

    half = bf16(dot(inv, src))
    edge = bf16(dot(cpl, half))
    slots = lax.broadcasted_iota(jnp.int32, (sum(sizes), tgt.shape[0]), 0)
    carried = dot(bf16(slots == tgt[None, :]), edge)
    ups = []
    for level, size in enumerate(sizes):
        for bit in range(2 * level, min(2 * level + 2, bits)):
            sent = partner(bf16(carried), 1 << bit)
            carried = carried + sent.astype(jnp.float32)
        up = both(bf16(dot(separators[level], both(bf16(carried[:size])))))
        ups.append(up)
        carried = carried[size:]
        if level < levels - 1:
            carried = carried.at[: sizes[level + 1]].add(dot(parents[level], up))
    own, down = [None] * levels, None
    for level in reversed(range(levels)):
        target = ups[level]
        if down is not None:
            target = bf16(target.astype(jnp.float32) - dot_tn(both(parents[level]), down))
        down = bf16(dot_tn(both(separators[level]), target))
        own[level] = lax.dynamic_slice_in_dim(down, lax.axis_index("sep") * sizes[level], sizes[level], 0)
    sep = jnp.concatenate(own, 0)
    lifted = bf16(dot_tn(cpl, jnp.take(sep, tgt, axis=0)))
    inner = bf16(dot_tn(inv, half) - dot_tn(inv, lifted))
    return (inner[None, None], sep[None, None])


def solution(mesh):
    whole = P("sub", "sep", None, None)
    placed = (whole,) * 2 + (whole, P("sub", "sep", None)) + (P("sub", "sep", None),) * 7
    two_stages = mesh.shape["sub"] == CHIPS * CHIPS
    return jax.shard_map(
        local if two_stages else local_any,
        mesh=mesh,
        in_specs=placed,
        out_specs=(whole, whole),
        check_vma=False,
    )
```

```python
import jax
import jax.numpy as jnp
from jax import lax
from jax.experimental import pallas as pl
from jax.experimental.pallas import tpu as pltpu
from jax.sharding import PartitionSpec as P

BLOCK = 256
CHIPS = 4
IN_PLANE = (3, 2, 1)
ALONG = (3, 2, 1)
AROUND = ((1, False), (3, True), (2, False))
MIB = 1024 * 1024
VMEM = pl.BlockSpec(memory_space=pltpu.VMEM)
HBM = pl.BlockSpec(memory_space=pltpu.HBM)


def bf16(x):
    return x.astype(jnp.bfloat16)


def dot(a, b):
    return jnp.dot(a, b, preferred_element_type=jnp.float32)


def dot_tn(a, b):
    return lax.dot_general(a, b, (((0,), (0,)), ((), ())), preferred_element_type=jnp.float32)


def call(kernel, name, outs, ins, specs, out_specs, flops, limit=16, scratch=()):
    ins = [pltpu.with_memory_space_constraint(x, pltpu.HBM) if s is HBM else x for x, s in zip(ins, specs)]
    moved = sum(x.size * x.dtype.itemsize for x in ins)
    return pl.pallas_call(
        kernel,
        out_shape=outs,
        in_specs=specs,
        out_specs=out_specs,
        scratch_shapes=list(scratch),
        compiler_params=pltpu.CompilerParams(vmem_limit_bytes=limit * MIB),
        cost_estimate=pl.CostEstimate(flops=flops, bytes_accessed=moved, transcendentals=0),
        name=name,
    )(*ins)


def in_plane():
    return lax.rem(lax.axis_index("sub"), CHIPS)


def struct(shape, dtype=jnp.bfloat16):
    return jax.ShapeDtypeStruct(shape, dtype)


def offsets(sizes):
    return [sum(sizes[:i]) for i in range(len(sizes))]


def places(sizes):
    return [sum(sizes[i + 1 :]) for i in range(len(sizes))]


def moved_rows(tgt, sizes, order):
    moved = tgt
    for start, place, size in zip(offsets(sizes), order, sizes):
        inside = (tgt >= start) & (tgt < start + size)
        moved = jnp.where(inside, tgt + (place - start), moved)
    return moved


def scatter_matrix(moved, rows, start=0):
    slots = lax.broadcasted_iota(jnp.int32, (rows, moved.shape[1]), 0)
    return bf16(jnp.where(slots + start == moved, 1.0, 0.0))


def leaf_forward(src, inv, cpl, tgt, separators, parents):
    inner, shots = src.shape
    count = inner // BLOCK
    sizes = [m.shape[0] for m in separators]
    s0, s1, s2, s3 = sizes
    o0, o1, o2, o3 = [m.shape[1] for m in separators]
    part, _ = share_rows(sizes)

    def kernel(src_hbm, inv_hbm, cpl_hbm, tgt_hbm, i0, i1, i2, i3, c0, c1, c2,
               half_ref, share0, share1, share2, share3, pack_ref,
               src, inv, cpl, edge_ref, small0, small1, tgt_ref, sems):
        moves = [(tgt_hbm, tgt_ref)]
        for i in range(count):
            rows = pl.ds(i * BLOCK, BLOCK)
            cols = pl.ds(0, (i + 1) * BLOCK)
            moves.append((src_hbm.at[rows], src.at[rows]))
            moves.append((inv_hbm.at[rows, cols], inv.at[rows, cols]))
            moves.append((cpl_hbm.at[:, rows], cpl.at[:, rows]))
        leaf = len(moves)
        moves += [
            (i0, small0),
            (c0, small1),
            (i3, pack_ref.at[pl.ds(0, s3), :]),
            (c2, pack_ref.at[pl.ds(s3, s3), pl.ds(0, o2)]),
            (i2, pack_ref.at[pl.ds(s3, s2), pl.ds(o2, o2)]),
            (c1, pack_ref.at[pl.ds(s3 + s2, s2), pl.ds(o2, o1)]),
            (i1, pack_ref.at[pl.ds(s3 + s2, s1), pl.ds(o2 + o1, o1)]),
        ]
        copies = [pltpu.make_async_copy(x, y, sems.at[i]) for i, (x, y) in enumerate(moves)]
        for copy in copies:
            copy.start()
        copies[0].wait()
        moved = moved_rows(tgt_ref[...], sizes, (CHIPS * part, s3 + s2, s3, 0))
        picks = [scatter_matrix(moved, part, part * (in_plane() ^ k)) for k in range(CHIPS)]
        picks = jnp.concatenate([*picks, scatter_matrix(moved, s0, CHIPS * part)], 0)
        for i in range(count):
            rows = pl.ds(i * BLOCK, BLOCK)
            cols = pl.ds(0, (i + 1) * BLOCK)
            copies[3 * i + 1].wait()
            copies[3 * i + 2].wait()
            half = bf16(dot(inv[rows, cols], src[cols, :]))
            half_ref[rows, :] = half
            copies[3 * i + 3].wait()
            term = dot(cpl[:, rows], half)
            if i == 0:
                edge_ref[...] = term
            else:
                edge_ref[...] += term
        edge = bf16(edge_ref[...])
        out = bf16(dot(picks, edge))
        for k, share in enumerate((share0, share1, share2, share3)):
            share[pl.ds(0, part), :] = out[k * part : (k + 1) * part]
            share[pl.ds(part, s0), :] = out[CHIPS * part :]
        for copy in copies[leaf:]:
            copy.wait()
        pack_ref[pl.ds(2 * s3, s0), pl.ds(0, o0)] = small0[...]
        pack_ref[pl.ds(s3 + s2 + s1, s1), pl.ds(o2 + o1, o0)] = small1[...]

    return call(
        kernel,
        "leaf_forward",
        (
            struct((inner, shots)),
            *[struct((part + s0, shots))] * CHIPS,
            struct((2 * s3 + s0, o3)),
        ),
        (src, inv, cpl, tgt, *separators, *parents),
        [HBM] * 11,
        (VMEM,) * (CHIPS + 2),
        600_000_000,
        scratch=[
            pltpu.VMEM(src.shape, jnp.bfloat16),
            pltpu.VMEM(inv.shape, jnp.bfloat16),
            pltpu.VMEM(cpl.shape, jnp.bfloat16),
            pltpu.VMEM((cpl.shape[0], shots), jnp.float32),
            pltpu.VMEM((s0, o0), jnp.bfloat16),
            pltpu.VMEM((s1, o0), jnp.bfloat16),
            pltpu.VMEM(tgt.shape, jnp.int32),
            pltpu.SemaphoreType.DMA((3 * count + 8,)),
        ],
    )


def share_rows(sizes):
    return sum(sizes[1:]) // CHIPS, sizes[1] // CHIPS


def ordered(first, own, other):
    return jnp.concatenate([jnp.where(first, own, other), jnp.where(first, other, own)], 0)


def plane_sum(pieces, pack, far_pack, separators, parents):
    sizes = [m.shape[0] for m in separators]
    s0, s1, s2, s3 = sizes
    o0, o1, o2, _ = [m.shape[1] for m in separators]
    part, side = share_rows(sizes)
    shots = pieces[0].shape[1]

    def kernel(a, b, c, d, pack_ref, far_pack_ref, share_ref, low_ref):
        first = lax.axis_index("sep") == 0
        total = sum(x[...].astype(jnp.float32) for x in (a, b, c, d))
        low = bf16(total[part:])
        low_ref[...] = low
        share_ref[pl.ds(0, part - s1), :] = bf16(total[: part - s1])
        inv_at = (pl.ds(2 * s3, s0), pl.ds(0, o0))
        cpl_at = (pl.ds(s3 + s2 + s1, s1), pl.ds(o2 + o1, o0))
        inv = ordered(first, pack_ref[inv_at], far_pack_ref[inv_at])
        up = bf16(dot(inv, ordered(first, low, jnp.zeros_like(low))))
        own, far = dot(pack_ref[cpl_at], up), dot(far_pack_ref[cpl_at], up)
        me = in_plane()
        end = total[part - s1 : part] + jnp.where(me == CHIPS - 1, own, 0.0)
        share_ref[pl.ds(part - s1, s1), :] = bf16(end)
        kept = far[:side]
        for q in range(1, CHIPS):
            kept = jnp.where(me == q, far[q * side : (q + 1) * side], kept)
        share_ref[pl.ds(part, side), :] = bf16(kept)

    return call(
        kernel,
        "plane_sum",
        (struct((part + side, shots)), struct((s0, shots))),
        (*pieces, pack, far_pack),
        [VMEM] * 6,
        (VMEM, VMEM),
        10_000_000,
        limit=4,
    )


def exchange_columns(cols):
    i = lax.broadcasted_iota(jnp.int32, (cols, cols), 0)
    j = lax.broadcasted_iota(jnp.int32, (cols, cols), 1)
    return bf16(jnp.where((i - j == cols // 2) | (j - i == cols // 2), 1.0, 0.0))


def solve_operator(pack, far_pack, separators, parents):
    s = [m.shape[0] for m in separators]
    o = [m.shape[1] for m in separators]
    total = sum(s)
    part, side = share_rows(s)
    width = CHIPS * (part + side)

    def share_order():
        i = lax.broadcasted_iota(jnp.int32, (width, width), 0)
        j = lax.broadcasted_iota(jnp.int32, (width, width), 1)
        q, r = j // (part + side), j % (part + side)
        from_ = jnp.where(r < part, q * part + r, CHIPS * part + q * side + r - part)
        return bf16(jnp.where(i == from_, 1.0, 0.0))

    def kernel(own_ref, far_ref, out_ref, far_out_ref, low_ref, levels, far_levels):
        first = lax.axis_index("sep") == 0

        def whole(row, rows, col, cols):
            at = (pl.ds(row, rows), pl.ds(col, cols))
            return ordered(first, own_ref[at], far_ref[at])

        def own_columns(x):
            half = x.shape[1] // 2
            if half % 128:
                return jnp.where(first, x, bf16(dot(x, exchange_columns(2 * half))))
            return jnp.where(first, x, jnp.concatenate([x[:, half:], x[:, :half]], 1))

        x3 = own_columns(whole(0, s[3], 0, o[3]))
        c2 = whole(s[3], s[3], 0, o[2])
        x2 = whole(s[3], s[2], o[2], o[2])
        c1 = whole(s[3] + s[2], s[2], o[2], o[1])
        x1 = whole(s[3] + s[2], s[1], o[2] + o[1], o[1])
        c0 = whole(s[3] + s[2] + s[1], s[1], o[2] + o[1], o[0])
        x0 = own_columns(whole(2 * s[3], s[0], 0, o[0]))
        t3 = bf16(dot(whole(0, s[3], 0, o[3]), c2))
        t2 = bf16(dot(x2, c1))
        t1 = bf16(dot(x1, c0))
        x2, x1 = own_columns(x2), own_columns(x1)
        n32 = bf16(dot(t3, x2))
        n21 = bf16(dot(t2, x1))
        n10 = bf16(dot(t1, x0))
        n31 = bf16(dot(t3, n21))
        n20 = bf16(dot(t2, n10))
        n30 = bf16(dot(t3, n20))

        def turned(x, sign):
            y = x.astype(jnp.float32).T
            return bf16(sign * y[: y.shape[0] // 2])

        m3 = jnp.concatenate([turned(x3, 1.0), turned(n32, -1.0), turned(n31, 1.0), turned(n30, -1.0)], 0)
        m2 = jnp.concatenate([turned(x2, 1.0), turned(n21, -1.0), turned(n20, 1.0)], 0)
        m1 = jnp.concatenate([turned(x1, 1.0), turned(n10, -1.0)], 0)
        m0 = turned(x0, 1.0)
        top, mid, low = s[3], s[3] + s[2], s[3] + s[2] + s[1]
        a3 = bf16(dot(m3, x3))
        levels[:, pl.ds(0, top)] = a3[:, :top]
        far_levels[:, pl.ds(0, top)] = a3[:, top:]
        a2 = dot(m3, n32)
        a2 = bf16(jnp.concatenate([a2[:top], a2[top:] + dot(m2, x2)], 0))
        levels[:, pl.ds(top, s[2])] = a2[:, : s[2]]
        far_levels[:, pl.ds(top, s[2])] = a2[:, s[2] :]
        a1 = dot(m3, n31)
        rest = a1[top:] + dot(m2, n21)
        a1 = bf16(jnp.concatenate([a1[:top], rest[: s[2]], rest[s[2] :] + dot(m1, x1)], 0))
        levels[:, pl.ds(mid, o[1])] = a1
        far_levels[:, pl.ds(mid, o[1])] = bf16(dot(a1, exchange_columns(o[1])))
        order = share_order()
        out_ref[...] = bf16(dot(levels[...], order))
        far_out_ref[...] = bf16(dot(far_levels[...], order))
        low_ref[pl.ds(0, low), :] = jnp.zeros((low, o[0]), jnp.bfloat16)
        low_ref[pl.ds(low, s[0]), :] = bf16(dot(m0, x0))

    shape = struct((total, width))
    return call(
        kernel,
        "solve_operator",
        (shape, shape, struct((total, o[0]))),
        (pack, far_pack),
        [VMEM] * 2,
        (VMEM,) * 3,
        1_000_000_000,
        scratch=[pltpu.VMEM((total, width), jnp.bfloat16)] * 2,
    )


def correction_operator(solve, far_solve, low_solve, lift, sizes):
    total, width = solve.shape
    inner = lift.shape[0]
    each = sum(share_rows(sizes))

    def kernel(solve_ref, far_ref, low_solve_ref, lift_ref, held_ref, other_ref, low_ref):
        for i, (mask, own) in enumerate(((0, True), *AROUND)):
            cols = pl.ds(i * each, each)
            at = pl.ds(pl.multiple_of((in_plane() ^ mask) * each, each), each)
            held_ref[pl.ds(0, total), cols] = (solve_ref if own else far_ref)[:, at]
            other_ref[pl.ds(0, total), cols] = (far_ref if own else solve_ref)[:, at]
        low_ref[pl.ds(0, total), :] = low_solve_ref[...]
        for ref in (held_ref, other_ref, low_ref):
            ref[pl.ds(total, inner), :] = bf16(-dot(lift_ref[...], ref[pl.ds(0, total), :]))

    shape = struct((total + inner, width))
    return call(
        kernel,
        "correction_operator",
        (shape, shape, struct((total + inner, low_solve.shape[1]))),
        (solve, far_solve, low_solve, lift),
        [VMEM] * 4,
        (VMEM,) * 3,
        1_000_000_000,
    )


def leaf_backward(inv, cpl, tgt, half, sizes):
    inner, shots = half.shape
    count = inner // BLOCK
    total = sum(sizes)

    def kernel(inv_ref, cpl_ref, tgt_ref, half_ref, direct_ref, lift_ref, reach_ref):
        onehot = scatter_matrix(moved_rows(tgt_ref[...], sizes, places(sizes)), total)
        for i in range(count):
            cols = pl.ds(i * BLOCK, BLOCK)
            reach_ref[:, cols] = bf16(dot(onehot, cpl_ref[:, cols]))
        for j in range(count):
            rows = pl.ds(j * BLOCK, inner - j * BLOCK)
            cols = pl.ds(j * BLOCK, BLOCK)
            block = inv_ref[rows, cols]
            direct_ref[cols, :] = dot_tn(block, half_ref[rows, :])
            lift_ref[cols, :] = bf16(dot(reach_ref[:, rows], block).T)

    return call(
        kernel,
        "leaf_backward",
        (struct((inner, shots), jnp.float32), struct((inner, total))),
        (inv, cpl, tgt, half),
        [VMEM] * 4,
        (VMEM, VMEM),
        1_000_000_000,
        scratch=[pltpu.VMEM((total, inner), jnp.bfloat16)],
    )


def own_part(held, low, far_low, operator, low_operator, direct, sizes):
    total = sum(sizes)
    inner, shots = direct.shape

    def kernel(held_ref, low_ref, far_low_ref, operator_ref, low_operator_ref, direct_ref, out_ref):
        low = jnp.concatenate([low_ref[...], far_low_ref[...]], 0)
        out = dot(operator_ref[...], held_ref[...]) + dot(low_operator_ref[...], low)
        out_ref[pl.ds(0, total), :] = out[:total]
        out_ref[pl.ds(total, inner), :] = out[total:] + direct_ref[...]

    return call(
        kernel,
        "own_part",
        struct((total + inner, shots), jnp.float32),
        (held, low, far_low, operator, low_operator, direct),
        [VMEM] * 6,
        VMEM,
        400_000_000,
    )


def finish(held, operator, own, sizes):
    total = sum(sizes)
    shots = held.shape[1]
    inner = own.shape[0] - total
    count = inner // BLOCK

    def kernel(held_ref, operator_ref, own_ref, inner_hbm, sep_hbm, inner_buf, sep_buf, sems):
        def block(start, size):
            rows = pl.ds(start, size)
            return bf16(own_ref[rows, :] + dot(operator_ref[rows, :], held_ref[...]))

        down = block(0, total)
        for begin, place, size in zip(offsets(sizes), places(sizes), sizes):
            sep_buf[pl.ds(begin, size), :] = down[place : place + size]
        copies = [pltpu.make_async_copy(sep_buf, sep_hbm, sems.at[count])]
        copies[0].start()
        for i in range(count):
            rows = pl.ds(i * BLOCK, BLOCK)
            inner_buf[rows, :] = block(total + i * BLOCK, BLOCK)
            copies.append(pltpu.make_async_copy(inner_buf.at[rows], inner_hbm.at[rows], sems.at[i]))
            copies[-1].start()
        for copy in copies:
            copy.wait()

    return call(
        kernel,
        "finish",
        (struct((inner, shots)), struct((total, shots))),
        (held, operator, own),
        [VMEM] * 3,
        (HBM, HBM),
        400_000_000,
        scratch=[
            pltpu.VMEM((inner, shots), jnp.bfloat16),
            pltpu.VMEM((total, shots), jnp.bfloat16),
            pltpu.SemaphoreType.DMA((count + 1,)),
        ],
    )


def other_strip(x):
    return lax.ppermute(x, "sep", [(0, 1), (1, 0)])


def partner(x, mask):
    return lax.ppermute(x, "sub", [(s, s ^ mask) for s in range(lax.axis_size("sub"))])


def shifted(x, planes):
    count = lax.axis_size("sub")
    return lax.ppermute(x, "sub", [(s, (s + CHIPS * planes) % count) for s in range(count)])


def partner_strip(x, mask):
    route = []
    for s in range(lax.axis_size("sub")):
        route += [(2 * s, 2 * (s ^ mask) + 1), (2 * s + 1, 2 * (s ^ mask))]
    return lax.ppermute(x, ("sub", "sep"), route)


def added(*terms):
    return bf16(sum(t.astype(jnp.float32) for t in terms))


def local(sources, inner_inv, coupling, boundary_map, *blocks):
    src, inv, cpl, tgt = sources[0, 0], inner_inv[0, 0], coupling[0, 0], boundary_map[0]
    separators = [m[0] for m in blocks[:4]]
    parents = [m[0] for m in blocks[4:]]
    sizes = [m.shape[0] for m in separators]
    half, *parts, pack = leaf_forward(src, inv, cpl, tgt, separators, parents)
    pieces = parts[:1] + [partner(parts[k], k) for k in IN_PLANE]
    direct, lift = leaf_backward(inv, cpl, tgt, half, sizes)
    far_pack = other_strip(pack)
    solve = solve_operator(pack, far_pack, separators, parents)
    pieces, solve = lax.optimization_barrier((pieces, solve))
    share, low = plane_sum(pieces, pack, far_pack, separators, parents)
    far_low = other_strip(low)
    along = [shifted(share, k) for k in ALONG]
    along, far_low, direct, lift = lax.optimization_barrier((along, far_low, direct, lift))
    share = added(share, *along)
    operators = correction_operator(*solve, lift, sizes)
    around = [partner(share, mask) if own else partner_strip(share, mask) for mask, own in AROUND]
    around, operators = lax.optimization_barrier((around, operators))
    held_operator, other_operator, low_operator = operators
    held = jnp.concatenate([share, *around], 0)
    own = own_part(held, low, far_low, held_operator, low_operator, direct, sizes)
    inner, sep = finish(other_strip(held), other_operator, own, sizes)
    return (inner[None, None], sep[None, None])


def local_any(sources, inner_inv, coupling, boundary_map, *blocks):
    src, inv, cpl, tgt = sources[0, 0], inner_inv[0, 0], coupling[0, 0], boundary_map[0, 0]
    separators = [m[0] for m in blocks[:4]]
    parents = [m[0] for m in blocks[4:]]
    sizes = [m.shape[0] for m in separators]
    levels = len(sizes)
    bits = lax.axis_size("sub").bit_length() - 1

    def both(x):
        return lax.all_gather(x, "sep", axis=0, tiled=True)

    half = bf16(dot(inv, src))
    edge = bf16(dot(cpl, half))
    slots = lax.broadcasted_iota(jnp.int32, (sum(sizes), tgt.shape[0]), 0)
    carried = dot(bf16(slots == tgt[None, :]), edge)
    ups = []
    for level, size in enumerate(sizes):
        for bit in range(2 * level, min(2 * level + 2, bits)):
            sent = partner(bf16(carried), 1 << bit)
            carried = carried + sent.astype(jnp.float32)
        up = both(bf16(dot(separators[level], both(bf16(carried[:size])))))
        ups.append(up)
        carried = carried[size:]
        if level < levels - 1:
            carried = carried.at[: sizes[level + 1]].add(dot(parents[level], up))
    own, down = [None] * levels, None
    for level in reversed(range(levels)):
        target = ups[level]
        if down is not None:
            target = bf16(target.astype(jnp.float32) - dot_tn(both(parents[level]), down))
        down = bf16(dot_tn(both(separators[level]), target))
        own[level] = lax.dynamic_slice_in_dim(down, lax.axis_index("sep") * sizes[level], sizes[level], 0)
    sep = jnp.concatenate(own, 0)
    lifted = bf16(dot_tn(cpl, jnp.take(sep, tgt, axis=0)))
    inner = bf16(dot_tn(inv, half) - dot_tn(inv, lifted))
    return (inner[None, None], sep[None, None])


def solution(mesh):
    whole = P("sub", "sep", None, None)
    placed = (whole,) * 2 + (whole, P("sub", "sep", None)) + (P("sub", "sep", None),) * 7
    two_stages = mesh.shape["sub"] == CHIPS * CHIPS
    return jax.shard_map(
        local if two_stages else local_any,
        mesh=mesh,
        in_specs=placed,
        out_specs=(whole, whole),
        check_vma=False,
    )
```
